256 devices in a mesh: span: 4 (over y), clip: 32 (over x, z), mp: 2 (over core).
Axes of the slice: x: 4, y: 4, z: 8, core: 2. Of those that a mesh axis runs over, the one named last changes fastest.
Arguments:
- queries: bfloat16 [32, 4, 512, 2560], P('clip', 'span', None, 'mp'), may hold values from -8 to 8
- keys: bfloat16 [32, 4, 512, 2560], P('clip', 'span', None, 'mp'), may hold values from -8 to 8
- values: bfloat16 [32, 4, 512, 2560], P('clip', 'span', None, 'mp'), may hold values from -6 to 6
- resid: bfloat16 [32, 4, 512, 5120], P('clip', 'span', None, 'mp'), may hold values from -4 to 4
- out_weight: bfloat16 [2560, 5120], P('clip', 'mp'), may hold values from -0.125 to 0.125
- gate_table: float32 [4, 5120], P(None, 'mp'), may hold values from 4 to 16
- step_scale: float32 [4], replicated, may hold values from 0.5 to 2
- gain: float32 [5120], P('mp'), may hold values from 0.5 to 1.5
- route: int32 [32, 4, 32, 1], P('clip', 'span'), may hold values from 0 to 31; in each aligned block of 32 rows (0 to 31, 32 to 63, ..., all dimensions but the last counted through in order) at most 2 rows name the same one
- clip_len: int32 [32], replicated, may hold values from 1 to 4
- tstep: int32 [32, 4], replicated, may hold values from 0 to 3
Outputs:
- scored: bfloat16 [4, 32, 32, 2, 16, 5120], P('span', 'clip', None, None, None, 'mp')
The draws below stay inside these ranges and needn't reach their ends.
Inputs may be any that keep to these rules, and one draw needn't show every extreme that they name: `route`: of the 32 blocks of one span, at most 2 go to one group, and some span sends exactly 2 to one group.
All inputs are finite; a program needn't handle non-finite values.
Results may differ from the reference program's by a relative error of at most 0.008.
Values may be sent and summed in bfloat16 or wider, within the bound.
A program may use at most 128 MiB of HBM per device.

```python
import math
import jax
import jax.numpy as jnp
import numpy as np
from jax import lax

D = 5120
HEADS = 20
HS = 128
TOKC = 512
NBLK = 32
NT = 4
HD = 2560
BROWS = 16
CLIPS = 32
SPANS = 4
CAP = 2


def draw_queries(key, part):
    key = jax.random.fold_in(key, 11)
    drawn = jnp.clip(jax.random.normal(key, (CLIPS, SPANS, TOKC, HEADS * HS), jnp.float32), -6.0, 6.0)
    return drawn.astype(jnp.bfloat16)


def draw_keys(key, part):
    key = jax.random.fold_in(key, 12)
    drawn = jnp.clip(jax.random.normal(key, (CLIPS, SPANS, TOKC, HEADS * HS), jnp.float32), -6.0, 6.0)
    return drawn.astype(jnp.bfloat16)


def with_ends(result, key, least, top_value):
    longest = result.shape.index(max(result.shape))
    spots = []
    for shift in (0, 1):
        where = [jax.random.randint(jax.random.fold_in(key, axis), (), 0, length) for axis, length in enumerate(result.shape)]
        where[longest] = (where[longest] + shift) % result.shape[longest]
        spots.append(tuple(where))
    return result.at[spots[0]].set(least).at[spots[1]].set(top_value)


def block_scale(key, shape, shards, least, largest):
    loudness = 1.0
    for axis_at, parts in shards:
        steps = jax.random.uniform(jax.random.fold_in(jax.random.fold_in(key, 6), axis_at), (parts,), jnp.float32, least / len(shards), largest / len(shards))
        loudness = loudness * jnp.repeat(jnp.exp(steps), shape[axis_at] // parts).reshape((-1,) + (1,) * (len(shape) - 1 - axis_at))
    return loudness


def assign_block(key, own, number, rows, count, top, bound, lean):
    order = jax.random.permutation(key, count)
    packed, ordinary = portions_of(count, rows * top, bound, lean, True), portions_of(count, rows * top, bound, lean, False)
    places = jnp.arange(count)

    def named(sizes, turn):
        used = int((sizes > 0).sum())
        fixed = max(1, used // 4)
        shifted = fixed + (places - fixed + turn * (used - fixed)) % max(1, count - fixed)
        return jnp.zeros((count,), jnp.int32).at[order[jnp.where(places < fixed, places, shifted)]].set(jnp.asarray(sizes, jnp.int32))

    sizes = jnp.where(number % 4 == 0, named(packed, number // 4), named(ordinary, number - number // 4 - 1))
    mixed = jax.random.permutation(jax.random.fold_in(own, 3), count)
    giver, taker = mixed[0:count // 2 * 2:2], mixed[1:count // 2 * 2:2]
    margin = jnp.minimum(sizes[giver] - 1, bound - sizes[taker]) // 2
    margin = jnp.where((giver == order[0]) | (taker == order[0]) | (sizes[taker] == 0), 0, jnp.maximum(margin, 0))
    shifted = jax.random.randint(jax.random.fold_in(own, 4), (count // 2,), 0, 1 << 20) % (margin + 1)
    sizes = sizes.at[giver].add(-shifted).at[taker].add(shifted)
    members = jnp.searchsorted(jnp.cumsum(sizes), jnp.arange(rows * top), side="right").astype(jnp.int32)
    grid = members.reshape(top, rows).T
    grid = grid[jax.random.permutation(jax.random.fold_in(own, 1), rows)]
    turn = jax.random.randint(jax.random.fold_in(own, 2), (rows, 1), 0, top)
    return jnp.take_along_axis(grid, (jnp.arange(top)[None, :] + turn) % top, axis=1)


def portions_of(amount, total, reach, skew, full):
    weights = [(1 << 20) // math.isqrt(rank ** skew) + 1 for rank in range(1, amount + 1)]
    largest = reach if full else min(reach, max(-(-total // amount), total * weights[0] // sum(weights)))
    least = 1 if total - largest >= amount - 1 else 0
    holding, spare = [largest] + [least] * (amount - 1), total - largest - least * (amount - 1)
    while spare > 0:
        movable = [i for i in range(1, amount) if holding[i] < largest] or [i for i in range(1, amount) if holding[i] < reach]
        mass, budget = sum([weights[i] for i in movable]), spare
        for i in movable:
            addition = min(reach - holding[i], max(1, budget * weights[i] // mass), spare)
            holding[i] = holding[i] + addition
            spare = spare - addition
    return np.array(holding)


def bell_draw(rng, shape, scale, limit, cuts=(), kind=jnp.bfloat16):
    result = scale * jax.random.normal(rng, shape, jnp.float32)
    if cuts:
        result = result * block_scale(rng, shape, cuts, -0.22, 0.18)
    return jnp.clip(result, -limit, limit).astype(kind)


def setup_inputs(seed: int = 0) -> dict:
    splits = jax.random.split(jax.random.key(seed), 12)
    queries = draw_queries(jax.random.fold_in(splits[11], 71), 0)
    keys = draw_keys(jax.random.fold_in(splits[11], 71), 0)
    values = bell_draw(splits[2], (CLIPS, SPANS, TOKC, HD), 1.0, 6.0, ((0, 32), (1, 4), (3, 2)))
    resid = bell_draw(splits[3], (CLIPS, SPANS, TOKC, D), 0.5, 4.0, ((0, 32), (1, 4), (3, 2)))
    out_weight = bell_draw(splits[4], (HD, D), HD ** -0.5, 0.125, ((0, 32), (1, 2)))
    gate_table = jnp.clip(jnp.exp(math.log(16.0) - 1.3862944 * jax.random.uniform(splits[5], (NT, D), jnp.float32) ** block_scale(splits[5], (NT, D), ((1, 2),), -0.2, 0.2)), 4.0, 16.0)
    step_scale = jnp.clip(jnp.exp(jax.random.uniform(splits[6], (NT,), jnp.float32, math.log(0.5), math.log(2.0))), 0.5, 2.0)
    gain = jnp.clip(1.0 + 0.1 * jax.random.normal(splits[7], (D,), jnp.float32), 0.5, 1.5)
    route_keys = jax.random.split(jax.random.fold_in(splits[8], 1), CLIPS * SPANS * NBLK // NBLK)
    route_turns = jax.random.permutation(jax.random.fold_in(splits[8], 3), CLIPS * SPANS * NBLK // NBLK)
    route = jax.vmap(lambda own, number: assign_block(jax.random.fold_in(splits[8], 2), own, number, NBLK, CLIPS, 1, CAP, 2))(route_keys, route_turns).reshape((CLIPS, SPANS, NBLK, 1))
    clip_len = with_ends(jax.random.randint(splits[9], (CLIPS,), 1, SPANS + 1), jax.random.fold_in(splits[9], 1), 1, SPANS).astype(jnp.int32)
    tstep = with_ends(jax.random.randint(splits[10], (CLIPS, SPANS), 0, NT), jax.random.fold_in(splits[10], 1), 0, NT - 1).astype(jnp.int32)
    return dict(queries=queries, keys=keys, values=values, resid=resid, out_weight=out_weight, gate_table=gate_table, step_scale=step_scale, gain=gain, route=route, clip_len=clip_len, tstep=tstep)


def one_clip(items, out_weight, gate_table, step_scale, gain):
    query, key_all, val_all, resid_clip, dest_clip, length, steps = items
    inv = 1.0 / math.sqrt(HS)
    groups = jnp.arange(CLIPS, dtype=jnp.int32)
    outs = []
    for span in range(SPANS):
        q_heads = query[span].reshape(TOKC, HEADS, HS).astype(jnp.float32)
        k_heads = key_all[:span + 1].reshape((span + 1) * TOKC, HEADS, HS).astype(jnp.float32)
        v_heads = val_all[:span + 1].reshape((span + 1) * TOKC, HEADS, HS).astype(jnp.float32)
        scores = jnp.einsum('qhd,khd->hqk', q_heads, k_heads) * inv
        top = lax.optimization_barrier(jnp.max(scores, axis=-1, keepdims=True))
        prob = jnp.exp(scores - top)
        weights = prob.astype(jnp.bfloat16).astype(jnp.float32)
        total = lax.optimization_barrier(jnp.sum(prob, axis=-1))
        mixed = jnp.einsum('hqk,khd->qhd', weights, v_heads) / jnp.transpose(total)[:, :, None]
        attn = mixed.reshape(TOKC, HD).astype(jnp.bfloat16)
        proj = jnp.dot(attn, out_weight, preferred_element_type=jnp.float32)
        step = steps[span]
        row = (resid_clip[span].astype(jnp.float32) + gate_table[step] * proj).astype(jnp.bfloat16)
        row = lax.optimization_barrier(row)
        live = jnp.where(span < length, 1.0, 0.0).astype(jnp.float32)
        factor = step_scale[step] * live
        value = (row.astype(jnp.float32) * factor * gain).astype(jnp.bfloat16)
        blocks = value.reshape(NBLK, BROWS, D)
        dest = dest_clip[span, :, 0]
        onehot = (dest[:, None] == groups[None, :]).astype(jnp.int32)
        before = jnp.cumsum(onehot, axis=0) - onehot
        rank = lax.optimization_barrier(jnp.sum(before * onehot, axis=1)).astype(jnp.int32)
        buffer = jnp.zeros((CLIPS, CAP, BROWS, D), jnp.bfloat16).at[dest, rank].set(blocks)
        outs.append(buffer)
    return jnp.stack(outs)

def reference(queries, keys, values, resid, out_weight, gate_table, step_scale, gain, route, clip_len, tstep):
    per_clip = lax.map(lambda items: one_clip(items, out_weight, gate_table, step_scale, gain), (queries, keys, values, resid, route, clip_len, tstep))
    return jnp.transpose(per_clip, (1, 2, 0, 3, 4, 5))
```

```python
import functools
import math

import jax
import jax.numpy as jnp
from jax import lax
from jax.experimental import pallas as pl
from jax.experimental.pallas import tpu as pltpu
from jax.sharding import PartitionSpec as P

MESH = pl.DeviceIdType.MESH
HS = 128
NX, NZ, NY = 4, 8, 4
NCLIP = 32
TOK = 512
NB = 32
BR = 16
HALF = 1280
INNER = 2560
WID = 2560
SHARD = 80
MAXH = 3
CA = 768
PART = {
    "A": ((0, CA), (0, CA // 2), (CA // 2, CA)),
    "B": ((CA, WID), (CA, (CA + WID) // 2), ((CA + WID) // 2, WID)),
}
CHUNKS = ((0, 256, "A"), (256, 768, "A"), (768, 1280, "B"), (1280, 1792, "B"), (1792, 2304, "B"), (2304, 2560, "B"))


def plan():
    names = []
    for way in (1, -1):
        for hop in (1, 2, 3, 4):
            names.append(("Bz", way, hop))
        for hop in (1, 2):
            names.append(("Ax", way, hop))
        for hop in (1, 2, 3, 4):
            for xrel in (0, -1, 1, 2):
                names.append(("Az", way, hop, xrel))
        for hop in (1, 2):
            for zrel in (0, -1, 1, -2, 2, -3, 3, 4):
                names.append(("Bx", way, hop, zrel))
    return {name: at for at, name in enumerate(names)}


NAMES = plan()


def kernel(
    q_ref, k_ref, v_ref, resid_ref, w_ref, gate_ref, gain_ref, scale_ref, route_ref, len_ref, step_ref,
    out_ref,
    qkv, obuf, feats, wfull, resid_v, valbuf, sendbuf, inv,
    q_send, q_recv, o_send, o_recv, sib_send, sib_recv, w_send, w_recv, w_own, r_sem, a_send, a_recv,
):
    y = lax.axis_index("span")
    cl = lax.axis_index("clip")
    m = lax.axis_index("mp")
    x = cl // NZ
    z = lax.rem(cl, NZ)

    def clip_at(dx, dz):
        return lax.rem(x + (dx + NX), NX) * NZ + lax.rem(z + (dz + NZ), NZ)

    def first_head(yy):
        return (5 * yy + 1 - m) // 2

    def has_head(yy, i):
        return first_head(yy) + i < first_head(yy + 1)

    def cols128(at):
        return pl.ds(pl.multiple_of(at * HS, HS), HS)

    def remote(src, dst, send, recv, target):
        return pltpu.make_async_remote_copy(
            src_ref=src, dst_ref=dst, send_sem=send, recv_sem=recv, device_id=target, device_id_type=MESH
        )

    barrier = pltpu.get_barrier_semaphore()

    def greet(d, carry):
        pl.semaphore_signal(
            barrier, inc=1, device_id=(y, lax.rem(cl + d, NCLIP), m), device_id_type=MESH
        )
        return carry

    lax.fori_loop(1, NCLIP, greet, 0)
    for d in (1, 2, 3):
        pl.semaphore_signal(barrier, inc=1, device_id=(lax.rem(y + d, NY), cl, m), device_id_type=MESH)
    pl.semaphore_signal(barrier, inc=1, device_id=(y, cl, 1 - m), device_id_type=MESH)
    pl.semaphore_wait(barrier, NCLIP - 1 + 3 + 1)

    waited, sent = set(), []

    def rows_of(rel):
        return pl.ds(pl.multiple_of(clip_at(*rel) * SHARD, 16), SHARD)

    def w_start(name, rel, target, half=None, own=False):
        lo, hi = PART[name[0][0]][0 if half is None else 1 + half]
        dst = wfull.at[rows_of(rel), lo:hi]
        src = w_ref.at[:, lo:hi] if own else dst
        sent.append(hi - lo)
        remote(src, dst, w_send, w_recv.at[NAMES[name]], (y, clip_at(*target), m)).start()

    def w_wait(name, rel, half=None):
        if name in waited:
            return
        waited.add(name)
        lo, hi = PART[name[0][0]][0 if half is None else 1 + half]
        dst = wfull.at[rows_of(rel), lo:hi]
        remote(dst, dst, w_send, w_recv.at[NAMES[name]], (y, cl, m)).wait_recv()

    def half_of(way):
        return 0 if way == 1 else 1

    def bz_wait(way, hop):
        w_wait(("Bz", way, hop), (0, -way * hop), half_of(way) if hop == 4 else None)

    def ax_wait(way, hop):
        w_wait(("Ax", way, hop), (-way * hop, 0), half_of(way) if hop == 2 else None)

    def az_wait(way, hop, xrel):
        w_wait(("Az", way, hop, xrel), (xrel, -way * hop), half_of(way) if hop == 4 else None)

    def bx_wait(way, hop, zrel):
        w_wait(("Bx", way, hop, zrel), (-way * hop, zrel), half_of(way) if hop == 2 else None)

    def b_to_x(zrel, own=False):
        for way in (1, -1):
            w_start(("Bx", way, 1, zrel), (0, zrel), (way, 0), own=own)

    def a_to_z(xrel, own=False):
        for way in (1, -1):
            w_start(("Az", way, 1, xrel), (xrel, 0), (0, way), own=own)

    def bz_event(hop):
        for way in (1, -1):
            bz_wait(way, hop)
            if hop < 4:
                w_start(
                    ("Bz", way, hop + 1), (0, -way * hop), (0, way), half=half_of(way) if hop == 3 else None
                )
                b_to_x(-way * hop)
        if hop == 4:
            b_to_x(4)

    def ax_event(hop):
        for way in (1, -1):
            ax_wait(way, hop)
            if hop == 1:
                w_start(("Ax", way, 2), (-way, 0), (way, 0), half=half_of(way))
                a_to_z(-way)
        if hop == 2:
            a_to_z(2)

    def az_event(hop, xrel):
        for way in (1, -1):
            az_wait(way, hop, xrel)
            w_start(
                ("Az", way, hop + 1, xrel), (xrel, -way * hop), (0, way), half=half_of(way) if hop == 3 else None
            )

    def bx_event(zrel):
        for way in (1, -1):
            bx_wait(way, 1, zrel)
            w_start(("Bx", way, 2, zrel), (-way, zrel), (way, 0), half=half_of(way))

    def all_of(part):
        for way in (1, -1):
            if part == "A":
                for hop in (1, 2):
                    ax_wait(way, hop)
                for hop in (1, 2, 3, 4):
                    for xrel in (0, -1, 1, 2):
                        az_wait(way, hop, xrel)
            else:
                for hop in (1, 2, 3, 4):
                    bz_wait(way, hop)
                for hop in (1, 2):
                    for zrel in (0, -1, 1, -2, 2, -3, 3, 4):
                        bx_wait(way, hop, zrel)

    tensors = (q_ref, k_ref, v_ref)

    def qkv_out(i, d):
        yy = lax.rem(y + d, NY)

        @pl.when(has_head(yy, i))
        def _():
            for t in range(3):
                remote(
                    tensors[t].at[:, cols128(first_head(yy) + i)],
                    qkv.at[i, y, t],
                    q_send.at[i, d],
                    q_recv.at[i, y],
                    (yy, cl, m),
                ).start()

    def qkv_here(i):
        @pl.when(has_head(y, i))
        def _():
            for t in range(3):
                pltpu.make_async_copy(
                    tensors[t].at[:, cols128(first_head(y) + i)], qkv.at[i, y, t], q_recv.at[i, y]
                ).start()

    def qkv_sent(i, d):
        yy = lax.rem(y + d, NY)

        @pl.when(has_head(yy, i))
        def _():
            remote(qkv.at[i, 0], qkv.at[i, 0], q_send.at[i, d], q_recv.at[i, 0], (yy, cl, m)).wait_send()

    def own_cols(head):
        return cols128(m * (HALF // HS) + head)

    def to_sibling(head):
        part = feats.at[:, own_cols(head)]
        remote(part, part, sib_send, sib_recv, (y, cl, 1 - m)).start()

    rows_at_once = 256

    def attend(i, c):
        @pl.when(has_head(y, i))
        def _():
            pltpu.make_async_copy(qkv.at[i, c], qkv.at[i, c], q_recv.at[i, c]).wait()

            def tile(r, carry):
                rows = pl.ds(pl.multiple_of(r * rows_at_once, rows_at_once), rows_at_once)
                query = qkv[i, c, 0, rows, :]
                scores = [
                    lax.dot_general(
                        query, qkv[i, cc, 1], (((1,), (1,)), ((), ())), preferred_element_type=jnp.float32
                    )
                    for cc in range(c + 1)
                ]
                top = scores[0]
                for part in scores[1:]:
                    top = jnp.maximum(top, part)
                top = jnp.max(top, axis=1, keepdims=True)
                acc = jnp.zeros((rows_at_once, 2 * HS), jnp.float32)
                for cc in range(c + 1):
                    prob = jnp.exp((scores[cc] - top) * (1.0 / math.sqrt(HS))).astype(jnp.bfloat16)
                    val = jnp.concatenate([qkv[i, cc, 2], jnp.ones((TOK, HS), jnp.bfloat16)], axis=1)
                    acc = acc + jnp.dot(prob, val, preferred_element_type=jnp.float32)
                obuf[i, c, rows, :] = (acc[:, :HS] / acc[:, HS:]).astype(jnp.bfloat16)
                return carry

            lax.fori_loop(0, TOK // rows_at_once, tile, 0)
            head = first_head(y) + i

            @pl.when(y == c)
            def _():
                feats[:, own_cols(head)] = obuf[i, c]
                to_sibling(head)

            @pl.when(y != c)
            def _():
                remote(
                    obuf.at[i, c], feats.at[:, own_cols(head)], o_send.at[i, c], o_recv.at[head], (c, cl, m)
                ).start()

    def o_event(i):
        for d in (1, 2, 3):
            yy = lax.rem(y + d, NY)

            @pl.when(has_head(yy, i))
            def _(yy=yy):
                head = first_head(yy) + i
                part = feats.at[:, own_cols(head)]
                remote(part, part, o_send.at[i, 0], o_recv.at[head], (y, cl, m)).wait_recv()
                to_sibling(head)

    def find_slots():
        def of_group(g, carry):
            first, second, found = jnp.int32(NB), jnp.int32(NB), jnp.int32(0)
            for b in range(NB):
                here = route_ref[b] == g
                first = jnp.where(here & (found == 0), b, first)
                second = jnp.where(here & (found == 1), b, second)
                found = found + jnp.where(here, 1, 0)
            inv[2 * g] = first
            inv[2 * g + 1] = second
            return carry

        lax.fori_loop(0, NCLIP, of_group, 0)
        valbuf[NB] = jnp.zeros((BR, valbuf.shape[2]), jnp.bfloat16)

    w_start(("Bz", 1, 1), (0, 0), (0, 1), own=True)
    w_start(("Bz", -1, 1), (0, 0), (0, -1), own=True)
    for way in (1, -1):
        w_start(("Ax", way, 1), (0, 0), (way, 0), own=True)
    b_to_x(0, own=True)
    for i in range(MAXH):
        for d in (1, 3, 2):
            qkv_out(i, d)
        qkv_here(i)
        if i == 0:
            a_to_z(0, own=True)
    own_rows = wfull.at[rows_of((0, 0)), :]
    w_copy = pltpu.make_async_copy(w_ref, own_rows, w_own)
    w_copy.start()
    resid_copy = pltpu.make_async_copy(resid_ref, resid_v, r_sem)
    resid_copy.start()

    events = [(1.0, find_slots)]
    for hop, at in ((1, 6.0), (2, 12.0), (3, 18.0), (4, 22.0)):
        events.append((at, functools.partial(bz_event, hop)))
    for hop, at in ((1, 4.0), (2, 7.0)):
        events.append((at, functools.partial(ax_event, hop)))
    for hop in (1, 2, 3):
        for n, xrel in enumerate((0, -1, 1, 2)):
            events.append((18.0 + 10.0 * (hop - 1) + 2.5 * n, functools.partial(az_event, hop, xrel)))
    for n, zrel in enumerate((0, -1, 1, -2, 2, -3, 3, 4)):
        events.append((9.0 * (n + 1), functools.partial(bx_event, zrel)))
    for i in range(MAXH):
        for c in range(NY):
            events.append((13.0 * (i + 1) + 0.7 * c, functools.partial(attend, i, c)))
        events.append((13.0 * (i + 1) + (8.0 if i < 2 else 9.0), functools.partial(o_event, i)))
    events.sort(key=lambda item: item[0])
    begin = 48.5
    late = [act for at, act in events if at > begin]
    for at, act in events:
        if at <= begin:
            act()

    half_feats = feats.at[:, pl.ds(pl.multiple_of((1 - m) * HALF, HS), HALF)]
    remote(half_feats, half_feats, sib_send, sib_recv, (y, cl, 1 - m)).wait_recv()
    w_copy.wait()
    resid_copy.wait()

    step = step_ref[cl * NY + y]
    live = jnp.where(y < len_ref[cl], 1.0, 0.0).astype(jnp.float32)
    factor = scale_ref[step] * live

    def send_chunk(n, lo, hi):
        wide = hi - lo

        def tile(r, carry):
            rows = pl.ds(pl.multiple_of(r * rows_at_once, rows_at_once), rows_at_once)
            proj = jnp.dot(feats[rows, :], wfull[:, lo:hi], preferred_element_type=jnp.float32)
            gate = gate_ref[pl.ds(step, 1), lo:hi]
            row = (resid_v[rows, lo:hi].astype(jnp.float32) + gate * proj).astype(jnp.bfloat16)
            value = (row.astype(jnp.float32) * factor * gain_ref[:, lo:hi]).astype(jnp.bfloat16)
            many = rows_at_once // BR
            valbuf[pl.ds(r * many, many), :, :wide] = value.reshape(many, BR, wide)
            return carry

        lax.fori_loop(0, TOK // rows_at_once, tile, 0)

        def pack(g):
            for k in range(2):
                sendbuf[g, k, :, lo:hi] = valbuf[inv[2 * g + k], :, :wide]

        def send(d, carry):
            g = lax.rem(cl + d, NCLIP)
            pack(g)
            remote(
                sendbuf.at[g, :, :, lo:hi],
                out_ref.at[cl, :, :, lo:hi],
                a_send.at[n],
                a_recv.at[n],
                (y, g, m),
            ).start()
            return carry

        lax.fori_loop(1, NCLIP, send, 0)
        pack(cl)
        pltpu.make_async_copy(sendbuf.at[cl, :, :, lo:hi], out_ref.at[cl, :, :, lo:hi], a_recv.at[n]).start()

    for n, (lo, hi, part) in enumerate(CHUNKS):
        if part == "B":
            while late:
                late.pop(0)()
        all_of(part)
        send_chunk(n, lo, hi)
        for _ in range(2):
            if late:
                late.pop(0)()

    assert len(waited) == len(NAMES) and sum(sent) == (NCLIP - 1) * WID
    for n, (lo, hi, part) in enumerate(CHUNKS):
        most = sendbuf.at[0 : NCLIP - 1, :, :, lo:hi]
        remote(most, most, a_send.at[n], a_recv.at[n], (y, cl, m)).wait_send()
        whole = out_ref.at[:, :, :, lo:hi]
        pltpu.make_async_copy(whole, whole, a_recv.at[n]).wait()
    most = wfull.at[0 : (NCLIP - 1) * SHARD, :]
    remote(most, most, w_send, w_recv.at[0], (y, cl, m)).wait_send()
    for i in range(MAXH):
        for d in (1, 2, 3):
            qkv_sent(i, d)
        for c in range(NY):

            @pl.when(has_head(y, i) & (y != c))
            def _(i=i, c=c):
                remote(obuf.at[i, c], obuf.at[i, c], o_send.at[i, c], o_recv.at[0], (y, cl, m)).wait_send()

    remote(half_feats, half_feats, sib_send, sib_recv, (y, cl, 1 - m)).wait_send()


def shards(queries, keys, values, resid, out_weight, gate_table, step_scale, gain, route, clip_len, tstep):
    hbm = pl.BlockSpec(memory_space=pl.ANY)
    vmem = pl.BlockSpec(memory_space=pltpu.VMEM)
    smem = pl.BlockSpec(memory_space=pltpu.SMEM)
    dma = pltpu.SemaphoreType.DMA
    bf16 = jnp.bfloat16
    scored = pl.pallas_call(
        kernel,
        out_shape=jax.ShapeDtypeStruct((NCLIP, 2, BR, WID), bf16),
        in_specs=[hbm] * 5 + [vmem] * 2 + [smem] * 4,
        out_specs=hbm,
        scratch_shapes=[
            pltpu.VMEM((MAXH, NY, 3, TOK, HS), bf16),
            pltpu.VMEM((MAXH, NY, TOK, HS), bf16),
            pltpu.VMEM((TOK, INNER), bf16),
            pltpu.VMEM((INNER, WID), bf16),
            pltpu.VMEM((TOK, WID), bf16),
            pltpu.VMEM((NB + 1, BR, 512), bf16),
            pltpu.VMEM((NCLIP, 2, BR, WID), bf16),
            pltpu.SMEM((2 * NCLIP,), jnp.int32),
            dma((MAXH, NY)),
            dma((MAXH, NY)),
            dma((MAXH, NY)),
            dma((HALF // HS,)),
            dma,
            dma,
            dma,
            dma((len(NAMES),)),
            dma,
            dma,
            dma((len(CHUNKS),)),
            dma((len(CHUNKS),)),
        ],
        compiler_params=pltpu.CompilerParams(
            collective_id=0, has_side_effects=True, vmem_limit_bytes=56 * 1024 * 1024
        ),
        cost_estimate=pl.CostEstimate(flops=12_000_000_000, bytes_accessed=20_000_000, transcendentals=8_000_000),
    )(
        queries[0, 0],
        keys[0, 0],
        values[0, 0],
        resid[0, 0],
        out_weight,
        gate_table,
        gain[None, :],
        step_scale,
        route[0, 0, :, 0],
        clip_len,
        tstep.reshape(-1),
    )
    return scored[None, None]


def solution(mesh):
    placed = (
        P("clip", "span", None, "mp"),
        P("clip", "span", None, "mp"),
        P("clip", "span", None, "mp"),
        P("clip", "span", None, "mp"),
        P("clip", "mp"),
        P(None, "mp"),
        P(),
        P("mp"),
        P("clip", "span", None, None),
        P(),
        P(),
    )
    return jax.shard_map(
        shards,
        mesh=mesh,
        in_specs=placed,
        out_specs=P("span", "clip", None, None, None, "mp"),
        check_vma=False,
    )
```

```python
import functools
import math

import jax
import jax.numpy as jnp
from jax import lax
from jax.experimental import pallas as pl
from jax.experimental.pallas import tpu as pltpu
from jax.sharding import PartitionSpec as P

MESH = pl.DeviceIdType.MESH
HS = 128
NX, NZ, NY = 4, 8, 4
NCLIP = 32
TOK = 512
NB = 32
BR = 16
HALF = 1280
HEADS = 10
INNER = 2560
WID = 2560
SHARD = 80
MAXH = 3
CAP = 3
TAB = 2 * NCLIP + 16
CA = 1024
PART = {
    "A": ((0, CA), (0, CA // 2), (CA // 2, CA)),
    "B": ((CA, WID), (CA, (CA + WID) // 2), ((CA + WID) // 2, WID)),
}
CHUNK = 512
CHUNKS = tuple((lo, lo + CHUNK) for lo in range(0, WID, CHUNK))
ROWS = 256
ZRELS = (0, -1, 1, -2, 2, -3, 3, 4)
XRELS = (0, -1, 1, 2)


def plan():
    names = []
    for way in (1, -1):
        names += [("Bz", way, hop) for hop in (1, 2, 3, 4)]
        names += [("Ax", way, hop) for hop in (1, 2)]
        names += [("Az", way, hop, xrel) for hop in (1, 2, 3, 4) for xrel in XRELS]
        names += [("Bx", way, hop, zrel) for hop in (1, 2) for zrel in ZRELS]
    return {name: at for at, name in enumerate(names)}


NAMES = plan()
RING = {
    name: at
    for at, name in enumerate(
        [(way, hop, piece) for way in (1, -1) for hop in (1, 2, 3) for piece in (0, 1)] + [(1, 4, 0), (-1, 4, 1)]
    )
}


def remote(src, dst, send, recv, target):
    return pltpu.make_async_remote_copy(
        src_ref=src, dst_ref=dst, send_sem=send, recv_sem=recv, device_id=target, device_id_type=MESH
    )


def place():
    y = lax.axis_index("span")
    cl = lax.axis_index("clip")
    m = lax.axis_index("mp")
    return y, cl, m, cl // NZ, lax.rem(cl, NZ)


def tile_rows(r):
    return pl.ds(pl.multiple_of(r * ROWS, ROWS), ROWS)


def gather_kernel(
    q_ref, k_ref, v_ref, w_ref, route_ref,
    feats, wfull, table, codes, most_ref,
    qkv, obuf, tiles, ytiles,
    q_send, q_recv, o_send, o_recv, o_here, sib_send, sib_recv, w_send, w_recv, w_own,
    t_send, t_recv, y_send, y_recv,
):
    y, cl, m, x, z = place()

    def clip_at(dx, dz):
        return lax.rem(x + (dx + NX), NX) * NZ + lax.rem(z + (dz + NZ), NZ)

    def first_head(yy):
        return (5 * yy + 1 - m) // 2

    def has_head(yy, i):
        return first_head(yy) + i < first_head(yy + 1)

    def cols128(at):
        return pl.ds(pl.multiple_of(at * HS, HS), HS)

    barrier = pltpu.get_barrier_semaphore()

    def greet(d, carry):
        pl.semaphore_signal(
            barrier, inc=1, device_id=(y, lax.rem(cl + d, NCLIP), m), device_id_type=MESH
        )
        return carry

    lax.fori_loop(1, NCLIP, greet, 0)
    for d in (1, 2, 3):
        pl.semaphore_signal(barrier, inc=1, device_id=(lax.rem(y + d, NY), cl, m), device_id_type=MESH)
    pl.semaphore_signal(barrier, inc=1, device_id=(y, cl, 1 - m), device_id_type=MESH)
    pl.semaphore_wait(barrier, NCLIP - 1 + 3 + 1)

    waited, sent = set(), []

    def rows_of(rel):
        return pl.ds(pl.multiple_of(clip_at(*rel) * SHARD, 16), SHARD)

    def w_start(name, rel, target, half=None, own=False):
        lo, hi = PART[name[0][0]][0 if half is None else 1 + half]
        dst = wfull.at[rows_of(rel), lo:hi]
        src = w_ref.at[:, lo:hi] if own else dst
        sent.append(hi - lo)
        remote(src, dst, w_send, w_recv.at[NAMES[name]], (y, clip_at(*target), m)).start()

    def w_wait(name, rel, half=None):
        if name in waited:
            return
        waited.add(name)
        lo, hi = PART[name[0][0]][0 if half is None else 1 + half]
        dst = wfull.at[rows_of(rel), lo:hi]
        remote(dst, dst, w_send, w_recv.at[NAMES[name]], (y, cl, m)).wait_recv()

    def half_of(way):
        return 0 if way == 1 else 1

    def bz_wait(way, hop):
        w_wait(("Bz", way, hop), (0, -way * hop), half_of(way) if hop == 4 else None)

    def ax_wait(way, hop):
        w_wait(("Ax", way, hop), (-way * hop, 0), half_of(way) if hop == 2 else None)

    def az_wait(way, hop, xrel):
        w_wait(("Az", way, hop, xrel), (xrel, -way * hop), half_of(way) if hop == 4 else None)

    def bx_wait(way, hop, zrel):
        w_wait(("Bx", way, hop, zrel), (-way * hop, zrel), half_of(way) if hop == 2 else None)

    def b_to_x(zrel, own=False):
        for way in (1, -1):
            w_start(("Bx", way, 1, zrel), (0, zrel), (way, 0), own=own)

    def a_to_z(xrel, own=False):
        for way in (1, -1):
            w_start(("Az", way, 1, xrel), (xrel, 0), (0, way), own=own)

    def bz_event(hop):
        for way in (1, -1):
            bz_wait(way, hop)
            if hop < 4:
                w_start(
                    ("Bz", way, hop + 1), (0, -way * hop), (0, way), half=half_of(way) if hop == 3 else None
                )
                b_to_x(-way * hop)
        if hop == 4:
            b_to_x(4)

    def ax_event(hop):
        for way in (1, -1):
            ax_wait(way, hop)
            if hop == 1:
                w_start(("Ax", way, 2), (-way, 0), (way, 0), half=half_of(way))
                a_to_z(-way)
        if hop == 2:
            a_to_z(2)

    def az_event(hop, xrel):
        for way in (1, -1):
            az_wait(way, hop, xrel)
            w_start(
                ("Az", way, hop + 1, xrel), (xrel, -way * hop), (0, way), half=half_of(way) if hop == 3 else None
            )

    def bx_event(zrel):
        for way in (1, -1):
            bx_wait(way, 1, zrel)
            w_start(("Bx", way, 2, zrel), (-way, zrel), (way, 0), half=half_of(way))

    def all_rows():
        for way in (1, -1):
            for hop in (1, 2):
                ax_wait(way, hop)
                for zrel in ZRELS:
                    bx_wait(way, hop, zrel)
            for hop in (1, 2, 3, 4):
                bz_wait(way, hop)
                for xrel in XRELS:
                    az_wait(way, hop, xrel)

    tensors = (q_ref, k_ref, v_ref)

    def qkv_out(i, d):
        yy = lax.rem(y + d, NY)

        @pl.when(has_head(yy, i))
        def _():
            for t in range(3):
                remote(
                    tensors[t].at[:, cols128(first_head(yy) + i)],
                    qkv.at[i, y, t],
                    q_send.at[i, d],
                    q_recv.at[i, y],
                    (yy, cl, m),
                ).start()

    def qkv_here(i):
        @pl.when(has_head(y, i))
        def _():
            for t in range(3):
                pltpu.make_async_copy(
                    tensors[t].at[:, cols128(first_head(y) + i)], qkv.at[i, y, t], q_recv.at[i, y]
                ).start()

    def qkv_sent(i, d):
        yy = lax.rem(y + d, NY)

        @pl.when(has_head(yy, i))
        def _():
            remote(qkv.at[i, 0], qkv.at[i, 0], q_send.at[i, d], q_recv.at[i, 0], (yy, cl, m)).wait_send()

    def own_cols(head):
        return cols128(m * HEADS + head)

    def attend(i, c):
        @pl.when(has_head(y, i))
        def _():
            pltpu.make_async_copy(qkv.at[i, c], qkv.at[i, c], q_recv.at[i, c]).wait()

            def tile(r, carry):
                rows = tile_rows(r)
                query = qkv[i, c, 0, rows, :]
                scores = [
                    lax.dot_general(
                        query, qkv[i, cc, 1], (((1,), (1,)), ((), ())), preferred_element_type=jnp.float32
                    )
                    for cc in range(c + 1)
                ]
                top = scores[0]
                for part in scores[1:]:
                    top = jnp.maximum(top, part)
                top = jnp.max(top, axis=1, keepdims=True)
                to_two = 1.0 / (math.sqrt(HS) * math.log(2.0))
                acc = jnp.zeros((ROWS, 2 * HS), jnp.float32)
                for cc in range(c + 1):
                    prob = jnp.exp2((scores[cc] - top) * to_two).astype(jnp.bfloat16)
                    val = jnp.concatenate([qkv[i, cc, 2], jnp.ones((TOK, HS), jnp.bfloat16)], axis=1)
                    acc = acc + jnp.dot(prob, val, preferred_element_type=jnp.float32)
                obuf[i, c, rows, :] = (acc[:, :HS] / acc[:, HS:]).astype(jnp.bfloat16)
                return carry

            lax.fori_loop(0, TOK // ROWS, tile, 0)
            head = first_head(y) + i
            part = feats.at[:, own_cols(head)]

            @pl.when(y == c)
            def _():
                pltpu.make_async_copy(obuf.at[i, c], part, o_here.at[i]).start()
                remote(obuf.at[i, c], part, sib_send, sib_recv, (y, cl, 1 - m)).start()

            @pl.when(y != c)
            def _():
                remote(obuf.at[i, c], part, o_send.at[i, c], o_recv.at[head], (c, cl, m)).start()

    def o_event(i):
        for d in (1, 3, 2):
            yy = lax.rem(y + d, NY)

            @pl.when(has_head(yy, i))
            def _(yy=yy):
                head = first_head(yy) + i
                part = feats.at[:, own_cols(head)]
                remote(part, part, o_send.at[i, 0], o_recv.at[head], (y, cl, m)).wait_recv()
                remote(part, part, sib_send, sib_recv, (y, cl, 1 - m)).start()

    def find_slots():
        shape = tiles.shape[1:]
        row_at = lax.broadcasted_iota(jnp.int32, shape, 0)
        lane_at = lax.broadcasted_iota(jnp.int32, shape, 1)

        def of_group(g, carry):
            count, tile = carry
            first, second, found = jnp.int32(NB), jnp.int32(NB), jnp.int32(0)
            for b in range(NB):
                here = route_ref[b] == g
                first = jnp.where(here & (found == 0), b, first)
                second = jnp.where(here & (found == 1), b, second)
                found = found + jnp.where(here, 1, 0)
            table[2 * g] = first
            table[2 * g + 1] = second
            code = jnp.where((second < NB) & (count < CAP), count, CAP)
            tile = jnp.where((row_at == 0) & (lane_at == g), code, tile)
            return count + jnp.where(second < NB, 1, 0), tile

        count, tile = lax.fori_loop(0, NCLIP, of_group, (jnp.int32(0), jnp.zeros(shape, jnp.int32)))
        tiles[cl] = jnp.where(row_at == 1, count, tile)

        def extra(e, carry):
            def look(g, carry):
                at, seen = carry
                second = table[2 * g + 1]
                have = second < NB
                at = jnp.where(have & (seen == e), second, at)
                return at, seen + jnp.where(have, 1, 0)

            at, seen = lax.fori_loop(0, NCLIP, look, (jnp.int32(0), jnp.int32(0)))
            table[2 * NCLIP + e] = at
            return carry

        lax.fori_loop(0, TAB - 2 * NCLIP, extra, 0)

        def tell(d, carry):
            g = lax.rem(cl + d, NCLIP)
            remote(tiles.at[cl], tiles.at[cl], t_send, t_recv, (y, g, m)).start()
            return carry

        lax.fori_loop(1, NCLIP, tell, 0)

    def share_most():
        others = tiles.at[0 : NCLIP - 1]
        remote(others, others, t_send, t_recv, (y, cl, m)).wait_recv()
        codes[...] = tiles[:, 0, :]
        ytiles[y] = jnp.max(tiles[...], axis=0)
        for d in (1, 2, 3):
            remote(ytiles.at[y], ytiles.at[y], y_send.at[d], y_recv.at[y], (lax.rem(y + d, NY), cl, m)).start()

    def know_most():
        for d in (1, 2, 3):
            yy = lax.rem(y + d, NY)
            remote(ytiles.at[yy], ytiles.at[yy], y_send.at[d], y_recv.at[yy], (y, cl, m)).wait_recv()
        most_ref[...] = jnp.max(ytiles[...], axis=0)

    w_start(("Bz", 1, 1), (0, 0), (0, 1), own=True)
    w_start(("Bz", -1, 1), (0, 0), (0, -1), own=True)
    for way in (1, -1):
        w_start(("Ax", way, 1), (0, 0), (way, 0), own=True)
    b_to_x(0, own=True)
    for i in range(MAXH):
        for d in (1, 3, 2):
            qkv_out(i, d)
        qkv_here(i)
        if i == 0:
            a_to_z(0, own=True)
    w_copy = pltpu.make_async_copy(w_ref, wfull.at[rows_of((0, 0)), :], w_own)
    w_copy.start()

    events = [(1.0, find_slots), (24.0, share_most), (32.0, know_most)]
    for hop, at in ((1, 5.5), (2, 11.0), (3, 16.5), (4, 20.0)):
        events.append((at, functools.partial(bz_event, hop)))
    for hop, at in ((1, 4.0), (2, 7.0)):
        events.append((at, functools.partial(ax_event, hop)))
    for hop in (1, 2, 3):
        for n, xrel in enumerate(XRELS):
            events.append((17.0 + 13.0 * (hop - 1) + 3.3 * n, functools.partial(az_event, hop, xrel)))
    for n, zrel in enumerate(ZRELS):
        events.append((7.6 * (n + 1), functools.partial(bx_event, zrel)))
    for i, at, back in ((0, 17.0, 27.0), (1, 35.0, 45.0), (2, 50.0, 61.0)):
        for c in range(NY):
            events.append((at + 0.7 * c, functools.partial(attend, i, c)))
        events.append((back, functools.partial(o_event, i)))
    events.sort(key=lambda item: item[0])
    for at, act in events:
        act()
    all_rows()

    assert len(waited) == len(NAMES) and sum(sent) == (NCLIP - 1) * WID
    w_copy.wait()
    half_feats = feats.at[:, pl.ds(pl.multiple_of((1 - m) * HALF, HS), HALF)]
    remote(half_feats, half_feats, sib_send, sib_recv, (y, cl, 1 - m)).wait()
    most = wfull.at[0 : (NCLIP - 1) * SHARD, :]
    remote(most, most, w_send, w_recv.at[0], (y, cl, m)).wait_send()
    others = tiles.at[0 : NCLIP - 1]
    remote(others, others, t_send, t_recv, (y, cl, m)).wait_send()
    for d in (1, 2, 3):
        remote(ytiles.at[0], ytiles.at[0], y_send.at[d], y_recv.at[0], (y, cl, m)).wait_send()
    for i in range(MAXH):
        for d in (1, 2, 3):
            qkv_sent(i, d)

        @pl.when(has_head(y, i))
        def _(i=i):
            part = feats.at[:, own_cols(first_head(y) + i)]
            pltpu.make_async_copy(obuf.at[i, 0], part, o_here.at[i]).wait()

        for c in range(NY):

            @pl.when(has_head(y, i) & (y != c))
            def _(i=i, c=c):
                remote(obuf.at[i, c], obuf.at[i, c], o_send.at[i, c], o_recv.at[0], (y, cl, m)).wait_send()


def greet_clips(y, cl, m):
    barrier = pltpu.get_barrier_semaphore()

    def greet(d, carry):
        pl.semaphore_signal(
            barrier, inc=1, device_id=(y, lax.rem(cl + d, NCLIP), m), device_id_type=MESH
        )
        return carry

    lax.fori_loop(1, NCLIP, greet, 0)
    return barrier


def load_all(feats_ref, w_ref, resid_ref, feats, wfull, resid, f_sem, w_sem, r_sem):
    pltpu.make_async_copy(feats_ref, feats, f_sem).start()
    loads = []
    for n, (lo, hi) in enumerate(CHUNKS):
        loads.append(pltpu.make_async_copy(w_ref.at[:, lo:hi], wfull.at[:, lo:hi], w_sem.at[n]))
        loads[n].start()
        if n == 0:
            pltpu.make_async_copy(resid_ref, resid, r_sem).start()
    ready = set()

    def wait(n):
        if not ready:
            pltpu.make_async_copy(feats_ref, feats, f_sem).wait()
            pltpu.make_async_copy(resid_ref, resid, r_sem).wait()
        if n not in ready:
            ready.add(n)
            loads[n].wait()

    return wait


def values_of(feat, resid, wfull, gate_ref, gain_ref, step, factor, lo, hi):
    proj = jnp.dot(feat, wfull[:, lo:hi], preferred_element_type=jnp.float32)
    gate = gate_ref[pl.ds(step, 1), lo:hi]
    row = (resid.astype(jnp.float32) + gate * proj).astype(jnp.bfloat16)
    return (row.astype(jnp.float32) * factor * gain_ref[:, lo:hi]).astype(jnp.bfloat16)


def step_and_factor(step_ref, len_ref, scale_ref, cl, y):
    step = step_ref[cl * NY + y]
    live = jnp.where(y < len_ref[cl], 1.0, 0.0).astype(jnp.float32)
    return step, scale_ref[step] * live


def project(valbuf, feats, resid, wfull, gate_ref, gain_ref, step, factor, lo, hi):
    many = ROWS // BR

    def tile(r, carry):
        blocks = pl.ds(r * many, many)
        value = values_of(
            feats[blocks].reshape(ROWS, INNER),
            resid[blocks, :, lo:hi].reshape(ROWS, hi - lo),
            wfull, gate_ref, gain_ref, step, factor, lo, hi,
        )
        valbuf[blocks] = value.reshape(many, BR, hi - lo)
        return carry

    lax.fori_loop(0, TOK // ROWS, tile, 0)


def padded_kernel(
    feats_ref, w_ref, resid_ref, gate_ref, gain_ref, scale_ref, table, codes, len_ref, step_ref,
    out_ref,
    feats, wfull, resid, valbuf, sendbuf,
    f_sem, w_sem, r_sem, a_send, a_recv,
):
    y, cl, m, x, z = place()
    barrier = greet_clips(y, cl, m)
    wait = load_all(feats_ref, w_ref, resid_ref, feats, wfull, resid, f_sem, w_sem, r_sem)
    step, factor = step_and_factor(step_ref, len_ref, scale_ref, cl, y)
    valbuf[NB] = jnp.zeros((BR, CHUNK), jnp.bfloat16)
    for n, (lo, hi) in enumerate(CHUNKS):
        wait(n)
        project(valbuf, feats, resid, wfull, gate_ref, gain_ref, step, factor, lo, hi)
        if n == 0:
            pl.semaphore_wait(barrier, NCLIP - 1)

        def pack(g):
            for k in range(2):
                sendbuf[g, k, :, lo:hi] = valbuf[table[2 * g + k]]

        def send(d, carry):
            g = lax.rem(cl + d, NCLIP)
            pack(g)
            remote(
                sendbuf.at[g, :, :, lo:hi], out_ref.at[cl, :, :, lo:hi], a_send.at[n], a_recv.at[n], (y, g, m)
            ).start()
            return carry

        lax.fori_loop(1, NCLIP, send, 0)
        pack(cl)
        pltpu.make_async_copy(sendbuf.at[cl, :, :, lo:hi], out_ref.at[cl, :, :, lo:hi], a_recv.at[n]).start()
    for n, (lo, hi) in enumerate(CHUNKS):
        most = sendbuf.at[0 : NCLIP - 1, :, :, lo:hi]
        remote(most, most, a_send.at[n], a_recv.at[n], (y, cl, m)).wait_send()
        whole = out_ref.at[:, :, :, lo:hi]
        pltpu.make_async_copy(whole, whole, a_recv.at[n]).wait()


def short_kernel(
    feats_ref, w_ref, resid_ref, gate_ref, gain_ref, scale_ref, table, codes, len_ref, step_ref,
    out_ref,
    feats, wfull, resid, valbuf, sendbuf, featx, ext, stage, sendx,
    f_sem, w_sem, r_sem, a_send, a_recv, e_send, e_recv, x_send, x_recv,
):
    y, cl, m, x, z = place()
    barrier = greet_clips(y, cl, m)
    wait = load_all(feats_ref, w_ref, resid_ref, feats, wfull, resid, f_sem, w_sem, r_sem)
    step, factor = step_and_factor(step_ref, len_ref, scale_ref, cl, y)
    valbuf[NB] = jnp.zeros((BR, CHUNK), jnp.bfloat16)
    stage[CAP] = jnp.zeros((BR, WID), jnp.bfloat16)

    def firsts(n):
        lo, hi = CHUNKS[n]
        wait(n)
        project(valbuf, feats, resid, wfull, gate_ref, gain_ref, step, factor, lo, hi)
        if n == 0:
            pl.semaphore_wait(barrier, NCLIP - 1)

        def send(d, carry):
            g = lax.rem(cl + d, NCLIP)
            sendbuf[g, :, lo:hi] = valbuf[table[2 * g]]
            remote(
                sendbuf.at[g, :, lo:hi], out_ref.at[cl, 0, :, lo:hi], a_send.at[n], a_recv.at[n], (y, g, m)
            ).start()
            return carry

        lax.fori_loop(1, NCLIP, send, 0)
        sendbuf[cl, :, lo:hi] = valbuf[table[2 * cl]]
        pltpu.make_async_copy(sendbuf.at[cl, :, lo:hi], out_ref.at[cl, 0, :, lo:hi], a_recv.at[n]).start()

    pieces = ((0, WID // 2), (WID // 2, WID))

    def z_at(dz):
        return lax.rem(z + (dz + NZ), NZ)

    def ring_start(way, hop, piece):
        lo, hi = pieces[piece]
        part = ext.at[z_at(-way * (hop - 1)), :, :, lo:hi]
        remote(part, part, e_send, e_recv.at[RING[way, hop, piece]], (y, x * NZ + z_at(way), m)).start()

    def ring_wait(way, hop, piece):
        lo, hi = pieces[piece]
        part = ext.at[z_at(-way * hop), :, :, lo:hi]
        remote(part, part, e_send, e_recv.at[RING[way, hop, piece]], (y, cl, m)).wait_recv()

    def to_x(zrel):
        zs = z_at(zrel)
        source = x * NZ + zs
        stage[0:CAP] = ext[zs]
        for d in (1, 3, 2, 0):
            xx = lax.rem(x + d, NX)
            g = xx * NZ + z
            sendx[xx, zs] = stage[codes[source, g]]
            if d:
                remote(sendx.at[xx, zs], out_ref.at[source, 1], x_send, x_recv, (y, g, m)).start()
            else:
                pltpu.make_async_copy(sendx.at[xx, zs], out_ref.at[source, 1], x_recv).start()

    def seconds():
        blocks = [table[2 * NCLIP + e] for e in range(CAP)]
        for e in range(CAP):
            featx[e * BR : (e + 1) * BR, :] = feats[blocks[e]]
        for n, (lo, hi) in enumerate(CHUNKS):
            wait(n)
            left = jnp.concatenate([resid[blocks[e], :, lo:hi] for e in range(CAP)], axis=0)
            value = values_of(featx[...], left, wfull, gate_ref, gain_ref, step, factor, lo, hi)
            ext[z, :, :, lo:hi] = value.reshape(CAP, BR, hi - lo)
            for piece in (0, 1):
                if lo < pieces[piece][1] <= hi:
                    for way in (1, -1):
                        ring_start(way, 1, piece)
        to_x(0)

    def ring_event(hop):
        for piece in (0, 1):
            for way in (1, -1):
                if (way, hop, piece) in RING:
                    ring_wait(way, hop, piece)
                    if (way, hop + 1, piece) in RING:
                        ring_start(way, hop + 1, piece)
        if hop < 4:
            to_x(-hop)
            to_x(hop)
        else:
            to_x(4)

    firsts(0)
    seconds()
    firsts(1)
    ring_event(1)
    firsts(2)
    ring_event(2)
    firsts(3)
    ring_event(3)
    firsts(4)
    ring_event(4)

    for n, (lo, hi) in enumerate(CHUNKS):
        most = sendbuf.at[0 : NCLIP - 1, :, lo:hi]
        remote(most, most, a_send.at[n], a_recv.at[n], (y, cl, m)).wait_send()
        whole = out_ref.at[:, 0, :, lo:hi]
        pltpu.make_async_copy(whole, whole, a_recv.at[n]).wait()
    most = ext.at[0 : NZ - 1]
    remote(most, most, e_send, e_recv.at[0], (y, cl, m)).wait_send()
    most = sendx.at[0 : NX - 1]
    remote(most, most, x_send, x_recv, (y, cl, m)).wait_send()
    whole = out_ref.at[:, 1]
    pltpu.make_async_copy(whole, whole, x_recv).wait()


def shards(queries, keys, values, resid, out_weight, gate_table, step_scale, gain, route, clip_len, tstep):
    any_place = pl.BlockSpec(memory_space=pl.ANY)
    hbm = pl.BlockSpec(memory_space=pltpu.HBM)
    vmem = pl.BlockSpec(memory_space=pltpu.VMEM)
    smem = pl.BlockSpec(memory_space=pltpu.SMEM)
    dma = pltpu.SemaphoreType.DMA
    bf16, i32 = jnp.bfloat16, jnp.int32
    shape = jax.ShapeDtypeStruct
    feats, wfull, table, codes, most = pl.pallas_call(
        gather_kernel,
        out_shape=(
            shape((TOK, INNER), bf16),
            shape((INNER, WID), bf16),
            shape((TAB,), i32),
            shape((NCLIP, 128), i32),
            shape((8, 128), i32),
        ),
        in_specs=[hbm] * 4 + [smem],
        out_specs=(any_place, hbm, smem, vmem, vmem),
        scratch_shapes=[
            pltpu.VMEM((MAXH, NY, 3, TOK, HS), bf16),
            pltpu.VMEM((MAXH, NY, TOK, HS), bf16),
            pltpu.VMEM((NCLIP, 8, 128), i32),
            pltpu.VMEM((NY, 8, 128), i32),
            dma((MAXH, NY)),
            dma((MAXH, NY)),
            dma((MAXH, NY)),
            dma((HEADS,)),
            dma((MAXH,)),
            dma,
            dma,
            dma,
            dma((len(NAMES),)),
            dma,
            dma,
            dma,
            dma((NY,)),
            dma((NY,)),
        ],
        compiler_params=pltpu.CompilerParams(
            collective_id=0, has_side_effects=True, vmem_limit_bytes=58 * 1024 * 1024
        ),
        cost_estimate=pl.CostEstimate(flops=4_000_000_000, bytes_accessed=40_000_000, transcendentals=8_000_000),
    )(queries[0, 0], keys[0, 0], values[0, 0], out_weight, route[0, 0, :, 0])

    def exchange(kernel, number, scratch):
        return pl.pallas_call(
            kernel,
            out_shape=shape((NCLIP, 2, BR, WID), bf16),
            in_specs=[any_place, hbm, hbm] + [vmem] * 2 + [smem] * 5,
            out_specs=any_place,
            scratch_shapes=[
                pltpu.VMEM((NB, BR, INNER), bf16),
                pltpu.VMEM((INNER, WID), bf16),
                pltpu.VMEM((NB, BR, WID), bf16),
                pltpu.VMEM((NB + 1, BR, CHUNK), bf16),
            ]
            + scratch,
            compiler_params=pltpu.CompilerParams(
                collective_id=number, has_side_effects=True, vmem_limit_bytes=50 * 1024 * 1024
            ),
            cost_estimate=pl.CostEstimate(flops=7_000_000_000, bytes_accessed=30_000_000, transcendentals=0),
        )

    loads = [dma, dma((len(CHUNKS),)), dma]
    by_chunk = [dma((len(CHUNKS),)), dma((len(CHUNKS),))]
    short = exchange(
        short_kernel,
        1,
        [
            pltpu.VMEM((NCLIP, BR, WID), bf16),
            pltpu.VMEM((CAP * BR, INNER), bf16),
            pltpu.VMEM((NZ, CAP, BR, WID), bf16),
            pltpu.VMEM((CAP + 1, BR, WID), bf16),
            pltpu.VMEM((NX, NZ, BR, WID), bf16),
        ]
        + loads
        + by_chunk
        + [dma, dma((len(RING),)), dma, dma],
    )
    padded = exchange(padded_kernel, 2, [pltpu.VMEM((NCLIP, 2, BR, WID), bf16)] + loads + by_chunk)
    scored = lax.cond(
        most[1, 0] <= CAP,
        short,
        padded,
        feats.reshape(NB, BR, INNER),
        wfull,
        resid[0, 0].reshape(NB, BR, WID),
        gate_table,
        gain[None, :],
        step_scale,
        table,
        codes,
        clip_len,
        tstep.reshape(-1),
    )
    return scored[None, None]


def solution(mesh):
    placed = (
        P("clip", "span", None, "mp"),
        P("clip", "span", None, "mp"),
        P("clip", "span", None, "mp"),
        P("clip", "span", None, "mp"),
        P("clip", "mp"),
        P(None, "mp"),
        P(),
        P("mp"),
        P("clip", "span", None, None),
        P(),
        P(),
    )
    return jax.shard_map(
        shards,
        mesh=mesh,
        in_specs=placed,
        out_specs=P("span", "clip", None, None, None, "mp"),
        check_vma=False,
    )
```

```python
import functools
import math

import jax
import jax.numpy as jnp
from jax import lax
from jax.experimental import pallas as pl
from jax.experimental.pallas import tpu as pltpu
from jax.sharding import PartitionSpec as P

MESH = pl.DeviceIdType.MESH
HS = 128
NX, NZ, NY = 4, 8, 4
NCLIP = 32
TOK = 512
NB = 32
BR = 16
HALF = 1280
HEADS = 10
INNER = 2560
WID = 2560
SHARD = 80
MAXH = 3
CAP = 4
CA = 1024
PART = {
    "A": ((0, CA), (0, CA // 2), (CA // 2, CA)),
    "B": ((CA, WID), (CA, (CA + WID) // 2), ((CA + WID) // 2, WID)),
}
CHUNKS = ((0, 512, "A"), (512, 1024, "A"), (1024, 1536, "B"), (1536, 2048, "B"), (2048, 2560, "B"))
PIECES = ((0, CA), (CA, WID))
ROWS = 256
ZRELS = (0, -1, 1, -2, 2, -3, 3, 4)
XRELS = (0, -1, 1, 2)


def plan():
    names = []
    for way in (1, -1):
        names += [("Bz", way, hop) for hop in (1, 2, 3, 4)]
        names += [("Ax", way, hop) for hop in (1, 2)]
        names += [("Az", way, hop, xrel) for hop in (1, 2, 3, 4) for xrel in XRELS]
        names += [("Bx", way, hop, zrel) for hop in (1, 2) for zrel in ZRELS]
    return {name: at for at, name in enumerate(names)}


NAMES = plan()
RING = {
    name: at
    for at, name in enumerate(
        [(way, hop, piece) for way in (1, -1) for hop in (1, 2, 3) for piece in (0, 1)] + [(1, 4, 0), (-1, 4, 1)]
    )
}


def remote(src, dst, send, recv, target):
    return pltpu.make_async_remote_copy(
        src_ref=src, dst_ref=dst, send_sem=send, recv_sem=recv, device_id=target, device_id_type=MESH
    )


def place():
    y = lax.axis_index("span")
    cl = lax.axis_index("clip")
    m = lax.axis_index("mp")
    return y, cl, m, cl // NZ, lax.rem(cl, NZ)


def tile_rows(r):
    return pl.ds(pl.multiple_of(r * ROWS, ROWS), ROWS)


def main_kernel(
    q_ref, k_ref, v_ref, resid_ref, w_ref, gate_ref, gain_ref, scale_ref, route_ref, len_ref, step_ref,
    out_ref, values_ref, table, most_ref,
    qkv, obuf, feats, wfull, resid, valbuf, sendbuf, ext, stage, sendx, tiles, ytiles, codes, table_s, codes_s,
    q_send, q_recv, o_send, o_recv, sib_send, sib_recv, w_send, w_recv, w_own, r_sem, v_sem,
    t_send, t_recv, t_here, y_send, y_recv, a_send, a_recv, e_send, e_recv, x_send, x_recv,
):
    y, cl, m, x, z = place()

    def clip_at(dx, dz):
        return lax.rem(x + (dx + NX), NX) * NZ + lax.rem(z + (dz + NZ), NZ)

    def first_head(yy):
        return (5 * yy + 1 - m) // 2

    def has_head(yy, i):
        return first_head(yy) + i < first_head(yy + 1)

    def cols128(at):
        return pl.ds(pl.multiple_of(at * HS, HS), HS)

    barrier = pltpu.get_barrier_semaphore()

    def greet(d, carry):
        pl.semaphore_signal(
            barrier, inc=1, device_id=(y, lax.rem(cl + d, NCLIP), m), device_id_type=MESH
        )
        return carry

    lax.fori_loop(1, NCLIP, greet, 0)
    for d in (1, 2, 3):
        pl.semaphore_signal(barrier, inc=1, device_id=(lax.rem(y + d, NY), cl, m), device_id_type=MESH)
    pl.semaphore_signal(barrier, inc=1, device_id=(y, cl, 1 - m), device_id_type=MESH)
    pl.semaphore_wait(barrier, NCLIP - 1 + 3 + 1)

    waited, sent = set(), []

    def rows_of(rel):
        return pl.ds(pl.multiple_of(clip_at(*rel) * SHARD, 16), SHARD)

    def w_start(name, rel, target, half=None, own=False):
        lo, hi = PART[name[0][0]][0 if half is None else 1 + half]
        dst = wfull.at[rows_of(rel), lo:hi]
        src = w_ref.at[:, lo:hi] if own else dst
        sent.append(hi - lo)
        remote(src, dst, w_send, w_recv.at[NAMES[name]], (y, clip_at(*target), m)).start()

    def w_wait(name, rel, half=None):
        if name in waited:
            return
        waited.add(name)
        lo, hi = PART[name[0][0]][0 if half is None else 1 + half]
        dst = wfull.at[rows_of(rel), lo:hi]
        remote(dst, dst, w_send, w_recv.at[NAMES[name]], (y, cl, m)).wait_recv()

    def half_of(way):
        return 0 if way == 1 else 1

    def bz_wait(way, hop):
        w_wait(("Bz", way, hop), (0, -way * hop), half_of(way) if hop == 4 else None)

    def ax_wait(way, hop):
        w_wait(("Ax", way, hop), (-way * hop, 0), half_of(way) if hop == 2 else None)

    def az_wait(way, hop, xrel):
        w_wait(("Az", way, hop, xrel), (xrel, -way * hop), half_of(way) if hop == 4 else None)

    def bx_wait(way, hop, zrel):
        w_wait(("Bx", way, hop, zrel), (-way * hop, zrel), half_of(way) if hop == 2 else None)

    def b_to_x(zrel, own=False):
        for way in (1, -1):
            w_start(("Bx", way, 1, zrel), (0, zrel), (way, 0), own=own)

    def a_to_z(xrel, own=False):
        for way in (1, -1):
            w_start(("Az", way, 1, xrel), (xrel, 0), (0, way), own=own)

    def bz_event(hop):
        for way in (1, -1):
            bz_wait(way, hop)
            if hop < 4:
                w_start(
                    ("Bz", way, hop + 1), (0, -way * hop), (0, way), half=half_of(way) if hop == 3 else None
                )
                b_to_x(-way * hop)
        if hop == 4:
            b_to_x(4)

    def ax_event(hop):
        for way in (1, -1):
            ax_wait(way, hop)
            if hop == 1:
                w_start(("Ax", way, 2), (-way, 0), (way, 0), half=half_of(way))
                a_to_z(-way)
        if hop == 2:
            a_to_z(2)

    def az_event(hop, xrel):
        for way in (1, -1):
            az_wait(way, hop, xrel)
            w_start(
                ("Az", way, hop + 1, xrel), (xrel, -way * hop), (0, way), half=half_of(way) if hop == 3 else None
            )

    def bx_event(zrel):
        for way in (1, -1):
            bx_wait(way, 1, zrel)
            w_start(("Bx", way, 2, zrel), (-way, zrel), (way, 0), half=half_of(way))

    def all_of(part):
        for way in (1, -1):
            if part == "A":
                for hop in (1, 2):
                    ax_wait(way, hop)
                for hop in (1, 2, 3, 4):
                    for xrel in XRELS:
                        az_wait(way, hop, xrel)
            else:
                for hop in (1, 2, 3, 4):
                    bz_wait(way, hop)
                for hop in (1, 2):
                    for zrel in ZRELS:
                        bx_wait(way, hop, zrel)

    tensors = (q_ref, k_ref, v_ref)

    def qkv_out(i, d):
        yy = lax.rem(y + d, NY)

        @pl.when(has_head(yy, i))
        def _():
            for t in range(3):
                remote(
                    tensors[t].at[:, cols128(first_head(yy) + i)],
                    qkv.at[i, y, t],
                    q_send.at[i, d],
                    q_recv.at[i, y],
                    (yy, cl, m),
                ).start()

    def qkv_here(i):
        @pl.when(has_head(y, i))
        def _():
            for t in range(3):
                pltpu.make_async_copy(
                    tensors[t].at[:, cols128(first_head(y) + i)], qkv.at[i, y, t], q_recv.at[i, y]
                ).start()

    def qkv_sent(i, d):
        yy = lax.rem(y + d, NY)

        @pl.when(has_head(yy, i))
        def _():
            remote(qkv.at[i, 0], qkv.at[i, 0], q_send.at[i, d], q_recv.at[i, 0], (yy, cl, m)).wait_send()

    def own_cols(head):
        return cols128(m * HEADS + head)

    def attend(i, c):
        @pl.when(has_head(y, i))
        def _():
            pltpu.make_async_copy(qkv.at[i, c], qkv.at[i, c], q_recv.at[i, c]).wait()

            def tile(r, carry):
                rows = tile_rows(r)
                query = qkv[i, c, 0, rows, :]
                to_two = 1.0 / (math.sqrt(HS) * math.log(2.0))
                ones = jnp.ones((TOK, HS), jnp.bfloat16)
                top = jnp.full((ROWS, 1), -jnp.inf, jnp.float32)
                acc = jnp.zeros((ROWS, 2 * HS), jnp.float32)
                for cc in range(c + 1):
                    scores = lax.dot_general(
                        query, qkv[i, cc, 1], (((1,), (1,)), ((), ())), preferred_element_type=jnp.float32
                    )
                    higher = jnp.maximum(top, jnp.max(scores, axis=1, keepdims=True))
                    prob = jnp.exp2((scores - higher) * to_two).astype(jnp.bfloat16)
                    val = jnp.concatenate([qkv[i, cc, 2], ones], axis=1)
                    acc = acc * jnp.exp2((top - higher) * to_two)
                    acc = acc + jnp.dot(prob, val, preferred_element_type=jnp.float32)
                    top = higher
                many = ROWS // BR
                done = (acc[:, :HS] / acc[:, HS:]).astype(jnp.bfloat16)
                obuf[i, c, pl.ds(r * many, many)] = done.reshape(many, BR, HS)
                return carry

            lax.fori_loop(0, TOK // ROWS, tile, 0, unroll=True)
            head = first_head(y) + i
            part = feats.at[:, :, own_cols(head)]

            @pl.when(y == c)
            def _():
                feats[:, :, own_cols(head)] = obuf[i, c]
                remote(obuf.at[i, c], part, sib_send, sib_recv, (y, cl, 1 - m)).start()

            @pl.when(y != c)
            def _():
                remote(obuf.at[i, c], part, o_send.at[i, c], o_recv.at[head], (c, cl, m)).start()

    def o_event(i):
        for d in (1, 3, 2):
            yy = lax.rem(y + d, NY)

            @pl.when(has_head(yy, i))
            def _(yy=yy):
                head = first_head(yy) + i
                part = feats.at[:, :, own_cols(head)]
                remote(part, part, o_send.at[i, 0], o_recv.at[head], (y, cl, m)).wait_recv()
                remote(part, part, sib_send, sib_recv, (y, cl, 1 - m)).start()

    def find_slots():
        shape = tiles.shape[1:]
        row_at = lax.broadcasted_iota(jnp.int32, shape, 0)
        group = lax.broadcasted_iota(jnp.int32, shape, 1)
        first = jnp.full(shape, NB, jnp.int32)
        second = jnp.full(shape, NB, jnp.int32)
        for b in range(NB):
            here = group == route_ref[b]
            second = jnp.where(here & (first < NB) & (second == NB), b, second)
            first = jnp.where(here & (first == NB), b, first)
        have = jnp.where(second < NB, 1, 0)
        upto = have
        for shift in (1, 2, 4, 8, 16):
            upto = upto + jnp.where(group >= shift, pltpu.roll(upto, shift, 1), 0)
        before = upto - have
        total = jnp.sum(have, axis=1, keepdims=True)
        code = jnp.where((have == 1) & (before < CAP), before, CAP)
        extra = jnp.zeros(shape, jnp.int32)
        for e in range(CAP):
            at = jnp.sum(jnp.where((have == 1) & (before == e), second, 0), axis=1, keepdims=True)
            extra = jnp.where(group == e, at, extra)
        table[...] = jnp.where(row_at == 0, first, jnp.where(row_at == 1, second, extra))
        tiles[cl] = jnp.where(row_at == 0, code, total)

        def tell(d, carry):
            g = lax.rem(cl + d, NCLIP)
            remote(tiles.at[cl], tiles.at[cl], t_send, t_recv, (y, g, m)).start()
            return carry

        lax.fori_loop(1, NCLIP, tell, 0)
        table_copy.start()

    def share_most():
        others = tiles.at[0 : NCLIP - 1]
        remote(others, others, t_send, t_recv, (y, cl, m)).wait_recv()
        codes[...] = tiles[:, 0, :]
        codes_copy.start()
        ytiles[y] = jnp.max(tiles[...], axis=0)
        for d in (1, 2, 3):
            remote(ytiles.at[y], ytiles.at[y], y_send.at[d], y_recv.at[y], (lax.rem(y + d, NY), cl, m)).start()

    def know_most():
        for d in (1, 2, 3):
            yy = lax.rem(y + d, NY)
            remote(ytiles.at[yy], ytiles.at[yy], y_send.at[d], y_recv.at[yy], (y, cl, m)).wait_recv()
        most_ref[...] = jnp.max(ytiles[...], axis=0)

    table_copy = pltpu.make_async_copy(table, table_s, t_here.at[0])
    codes_copy = pltpu.make_async_copy(codes, codes_s, t_here.at[1])

    w_start(("Bz", 1, 1), (0, 0), (0, 1), own=True)
    w_start(("Bz", -1, 1), (0, 0), (0, -1), own=True)
    for way in (1, -1):
        w_start(("Ax", way, 1), (0, 0), (way, 0), own=True)
    b_to_x(0, own=True)
    for i in range(MAXH):
        for d in (1, 3, 2):
            qkv_out(i, d)
        qkv_here(i)
        if i == 0:
            a_to_z(0, own=True)
    w_copy = pltpu.make_async_copy(w_ref, wfull.at[rows_of((0, 0)), :], w_own)
    w_copy.start()
    resid_copy = pltpu.make_async_copy(resid_ref, resid, r_sem)
    resid_copy.start()
    valbuf[NB] = jnp.zeros((BR, WID), jnp.bfloat16)
    stage[CAP] = jnp.zeros((BR, WID), jnp.bfloat16)

    events = [(1.0, find_slots), (24.0, share_most), (32.0, know_most)]
    for hop, at in ((1, 5.5), (2, 11.0), (3, 16.5), (4, 20.0)):
        events.append((at, functools.partial(bz_event, hop)))
    for hop, at in ((1, 4.0), (2, 7.0)):
        events.append((at, functools.partial(ax_event, hop)))
    for hop in (1, 2, 3):
        for n, xrel in enumerate(XRELS):
            events.append((17.0 + 13.0 * (hop - 1) + 3.3 * n, functools.partial(az_event, hop, xrel)))
    for n, zrel in enumerate(ZRELS):
        events.append((7.6 * (n + 1), functools.partial(bx_event, zrel)))
    for i, at, back in ((0, 17.0, 27.0), (1, 35.0, 45.0), (2, 50.0, 61.0)):
        for c in range(NY):
            events.append((at + 0.7 * c, functools.partial(attend, i, c)))
        events.append((back, functools.partial(o_event, i)))
    events.sort(key=lambda item: item[0])
    late = [act for at, act in events if at > 61.0]
    for at, act in events:
        if at <= 61.0:
            act()

    half_feats = feats.at[:, :, pl.ds(pl.multiple_of((1 - m) * HALF, HS), HALF)]
    remote(half_feats, half_feats, sib_send, sib_recv, (y, cl, 1 - m)).wait_recv()
    w_copy.wait()
    resid_copy.wait()
    table_copy.wait()
    codes_copy.wait()

    step, factor = step_and_factor(step_ref, len_ref, scale_ref, cl, y)

    def project(n):
        lo, hi, part = CHUNKS[n]
        all_of(part)
        many = ROWS // BR

        def tile(r, carry):
            blocks = pl.ds(r * many, many)
            feat = feats[blocks].reshape(ROWS, INNER)
            proj = jnp.dot(feat, wfull[:, lo:hi], preferred_element_type=jnp.float32)
            gate = gate_ref[pl.ds(step, 1), lo:hi]
            left = resid[blocks, :, lo:hi].reshape(ROWS, hi - lo).astype(jnp.float32)
            row = (left + gate * proj).astype(jnp.bfloat16)
            value = (row.astype(jnp.float32) * factor * gain_ref[lo:hi].reshape(1, hi - lo)).astype(jnp.bfloat16)
            valbuf[blocks, :, lo:hi] = value.reshape(many, BR, hi - lo)
            return carry

        lax.fori_loop(0, TOK // ROWS, tile, 0)

    def firsts(n):
        lo, hi, part = CHUNKS[n]

        def send(d, carry):
            g = lax.rem(cl + d, NCLIP)
            sendbuf[g, :, lo:hi] = valbuf[table_s[0, g], :, lo:hi]
            remote(
                sendbuf.at[g, :, lo:hi], out_ref.at[cl, 0, :, lo:hi], a_send.at[n], a_recv.at[n], (y, g, m)
            ).start()
            return carry

        lax.fori_loop(1, NCLIP, send, 0)
        sendbuf[cl, :, lo:hi] = valbuf[table_s[0, cl], :, lo:hi]
        pltpu.make_async_copy(sendbuf.at[cl, :, lo:hi], out_ref.at[cl, 0, :, lo:hi], a_recv.at[n]).start()

    def z_at(dz):
        return lax.rem(z + (dz + NZ), NZ)

    def ring_start(way, hop, piece):
        lo, hi = PIECES[piece]
        part = ext.at[z_at(-way * (hop - 1)), :, :, lo:hi]
        remote(part, part, e_send, e_recv.at[RING[way, hop, piece]], (y, clip_at(0, way), m)).start()

    def ring_wait(way, hop, piece):
        lo, hi = PIECES[piece]
        part = ext.at[z_at(-way * hop), :, :, lo:hi]
        remote(part, part, e_send, e_recv.at[RING[way, hop, piece]], (y, cl, m)).wait_recv()

    def seconds(piece):
        lo, hi = PIECES[piece]
        for e in range(CAP):
            ext[z, e, :, lo:hi] = valbuf[table_s[2, e], :, lo:hi]
        for way in (1, -1):
            ring_start(way, 1, piece)

    def ring_event(hop, piece):
        for way in (1, -1):
            if (way, hop, piece) in RING:
                ring_wait(way, hop, piece)
                if (way, hop + 1, piece) in RING:
                    ring_start(way, hop + 1, piece)

    def to_x(zrel):
        zs = z_at(zrel)
        source = x * NZ + zs
        stage[0:CAP] = ext[zs]
        for d in (1, 3, 2, 0):
            xx = lax.rem(x + d, NX)
            g = xx * NZ + z
            sendx[xx, zs] = stage[codes_s[source, g]]
            if d:
                remote(sendx.at[xx, zs], out_ref.at[source, 1], x_send, x_recv, (y, g, m)).start()
            else:
                pltpu.make_async_copy(sendx.at[xx, zs], out_ref.at[source, 1], x_recv).start()

    def next_late(many):
        for _ in range(many):
            if late:
                late.pop(0)()

    project(0)
    firsts(0)
    next_late(1)
    project(1)
    seconds(0)
    firsts(1)
    next_late(len(late))
    project(2)
    project(3)
    project(4)
    seconds(1)
    values_copy = pltpu.make_async_copy(valbuf.at[0:NB], values_ref, v_sem)
    values_copy.start()
    to_x(0)
    ring_event(1, 0)
    firsts(2)
    ring_event(1, 1)
    to_x(1)
    to_x(-1)
    ring_event(2, 0)
    firsts(3)
    ring_event(2, 1)
    to_x(2)
    to_x(-2)
    ring_event(3, 0)
    firsts(4)
    ring_event(3, 1)
    to_x(3)
    to_x(-3)
    ring_event(4, 0)
    ring_event(4, 1)
    to_x(4)

    assert len(waited) == len(NAMES) and sum(sent) == (NCLIP - 1) * WID and not late
    for n, (lo, hi, part) in enumerate(CHUNKS):
        most = sendbuf.at[0 : NCLIP - 1, :, lo:hi]
        remote(most, most, a_send.at[n], a_recv.at[n], (y, cl, m)).wait_send()
        whole = out_ref.at[:, 0, :, lo:hi]
        pltpu.make_async_copy(whole, whole, a_recv.at[n]).wait()
    most = ext.at[0 : NZ - 1]
    remote(most, most, e_send, e_recv.at[0], (y, cl, m)).wait_send()
    most = sendx.at[0 : NX - 1]
    remote(most, most, x_send, x_recv, (y, cl, m)).wait_send()
    whole = out_ref.at[:, 1]
    pltpu.make_async_copy(whole, whole, x_recv).wait()
    values_copy.wait()
    remote(half_feats, half_feats, sib_send, sib_recv, (y, cl, 1 - m)).wait_send()
    most = wfull.at[0 : (NCLIP - 1) * SHARD, :]
    remote(most, most, w_send, w_recv.at[0], (y, cl, m)).wait_send()
    others = tiles.at[0 : NCLIP - 1]
    remote(others, others, t_send, t_recv, (y, cl, m)).wait_send()
    for d in (1, 2, 3):
        remote(ytiles.at[0], ytiles.at[0], y_send.at[d], y_recv.at[0], (y, cl, m)).wait_send()
    for i in range(MAXH):
        for d in (1, 2, 3):
            qkv_sent(i, d)
        for c in range(NY):

            @pl.when(has_head(y, i) & (y != c))
            def _(i=i, c=c):
                remote(obuf.at[i, c], obuf.at[i, c], o_send.at[i, c], o_recv.at[0], (y, cl, m)).wait_send()


def step_and_factor(step_ref, len_ref, scale_ref, cl, y):
    step = step_ref[y, cl]
    live = jnp.where(y < len_ref[cl], 1.0, 0.0).astype(jnp.float32)
    return step, scale_ref[step] * live


def second_kernel(values_ref, table, out_ref, valbuf, sendbuf, v_sem, a_send, a_recv):
    y, cl, m, x, z = place()
    barrier = pltpu.get_barrier_semaphore()

    def greet(d, carry):
        pl.semaphore_signal(
            barrier, inc=1, device_id=(y, lax.rem(cl + d, NCLIP), m), device_id_type=MESH
        )
        return carry

    lax.fori_loop(1, NCLIP, greet, 0)
    load = pltpu.make_async_copy(values_ref, valbuf.at[0:NB], v_sem)
    load.start()
    load.wait()
    valbuf[NB] = jnp.zeros((BR, WID), jnp.bfloat16)
    pl.semaphore_wait(barrier, NCLIP - 1)

    def send(d, carry):
        g = lax.rem(cl + d, NCLIP)
        sendbuf[g] = valbuf[table[1, g]]
        remote(sendbuf.at[g], out_ref.at[cl], a_send, a_recv, (y, g, m)).start()
        return carry

    lax.fori_loop(1, NCLIP, send, 0)
    sendbuf[cl] = valbuf[table[1, cl]]
    pltpu.make_async_copy(sendbuf.at[cl], out_ref.at[cl], a_recv).start()
    most = sendbuf.at[0 : NCLIP - 1]
    remote(most, most, a_send, a_recv, (y, cl, m)).wait_send()
    pltpu.make_async_copy(out_ref, out_ref, a_recv).wait()


def shards(queries, keys, values, resid, out_weight, gate_table, step_scale, gain, route, clip_len, tstep):
    any_place = pl.BlockSpec(memory_space=pl.ANY)
    hbm = pl.BlockSpec(memory_space=pltpu.HBM)
    vmem = pl.BlockSpec(memory_space=pltpu.VMEM)
    smem = pl.BlockSpec(memory_space=pltpu.SMEM)
    dma = pltpu.SemaphoreType.DMA
    bf16, i32 = jnp.bfloat16, jnp.int32
    shape = jax.ShapeDtypeStruct
    scored, rows, table, most = pl.pallas_call(
        main_kernel,
        out_shape=(
            shape((NCLIP, 2, BR, WID), bf16),
            shape((NB, BR, WID), bf16),
            shape((8, 128), i32),
            shape((8, 128), i32),
        ),
        in_specs=[hbm] * 5 + [vmem] * 2 + [smem] * 4,
        out_specs=(any_place, hbm, vmem, vmem),
        scratch_shapes=[
            pltpu.VMEM((MAXH, NY, 3, TOK, HS), bf16),
            pltpu.VMEM((MAXH, NY, NB, BR, HS), bf16),
            pltpu.VMEM((NB, BR, INNER), bf16),
            pltpu.VMEM((INNER, WID), bf16),
            pltpu.VMEM((NB, BR, WID), bf16),
            pltpu.VMEM((NB + 1, BR, WID), bf16),
            pltpu.VMEM((NCLIP, BR, WID), bf16),
            pltpu.VMEM((NZ, CAP, BR, WID), bf16),
            pltpu.VMEM((CAP + 1, BR, WID), bf16),
            pltpu.VMEM((NX, NZ, BR, WID), bf16),
            pltpu.VMEM((NCLIP, 8, 128), i32),
            pltpu.VMEM((NY, 8, 128), i32),
            pltpu.VMEM((NCLIP, 128), i32),
            pltpu.SMEM((8, 128), i32),
            pltpu.SMEM((NCLIP, 128), i32),
            dma((MAXH, NY)),
            dma((MAXH, NY)),
            dma((MAXH, NY)),
            dma((HEADS,)),
            dma,
            dma,
            dma,
            dma((len(NAMES),)),
            dma,
            dma,
            dma,
            dma,
            dma,
            dma((2,)),
            dma((NY,)),
            dma((NY,)),
            dma((len(CHUNKS),)),
            dma((len(CHUNKS),)),
            dma,
            dma((len(RING),)),
            dma,
            dma,
        ],
        compiler_params=pltpu.CompilerParams(
            collective_id=0, has_side_effects=True, vmem_limit_bytes=58 * 1024 * 1024
        ),
        cost_estimate=pl.CostEstimate(flops=11_000_000_000, bytes_accessed=40_000_000, transcendentals=8_000_000),
    )(
        queries[0, 0],
        keys[0, 0],
        values[0, 0],
        resid[0, 0].reshape(NB, BR, WID),
        out_weight,
        gate_table,
        gain,
        step_scale,
        route[0, 0, :, 0],
        clip_len,
        tstep.T,
    )

    def direct(scored, rows, table):
        second = pl.pallas_call(
            second_kernel,
            out_shape=shape((NCLIP, BR, WID), bf16),
            in_specs=[hbm, smem],
            out_specs=hbm,
            scratch_shapes=[
                pltpu.VMEM((NB + 1, BR, WID), bf16),
                pltpu.VMEM((NCLIP, BR, WID), bf16),
                dma,
                dma,
                dma,
            ],
            compiler_params=pltpu.CompilerParams(
                collective_id=1, has_side_effects=True, vmem_limit_bytes=16 * 1024 * 1024
            ),
        )(rows, table)
        return jnp.concatenate([scored[:, :1], second[:, None]], axis=1)

    scored = lax.cond(most[1, 0] <= CAP, lambda scored, rows, table: scored, direct, scored, rows, table)
    return scored[None, None]


def solution(mesh):
    placed = (
        P("clip", "span", None, "mp"),
        P("clip", "span", None, "mp"),
        P("clip", "span", None, "mp"),
        P("clip", "span", None, "mp"),
        P("clip", "mp"),
        P(None, "mp"),
        P(),
        P("mp"),
        P("clip", "span", None, None),
        P(),
        P(),
    )
    return jax.shard_map(
        shards,
        mesh=mesh,
        in_specs=placed,
        out_specs=P("span", "clip", None, None, None, "mp"),
        check_vma=False,
    )
```

```python
import functools
import math

import jax
import jax.numpy as jnp
from jax import lax
from jax.experimental import pallas as pl
from jax.experimental.pallas import tpu as pltpu
from jax.sharding import PartitionSpec as P

MESH = pl.DeviceIdType.MESH
HS = 128
NX, NZ, NY = 4, 8, 4
NCLIP = 32
TOK = 512
NB = 32
BR = 16
HALF = 1280
HEADS = 10
INNER = 2560
WID = 2560
SHARD = 80
MAXH = 3
CAP = 4
CA = 1024
PART = {
    "A": ((0, CA), (0, CA // 2), (CA // 2, CA)),
    "B": ((CA, WID), (CA, (CA + WID) // 2), ((CA + WID) // 2, WID)),
}
CHUNKS = ((0, 512, "A"), (512, 1024, "A"), (1024, 1536, "B"), (1536, 2048, "B"), (2048, 2560, "B"))
PIECES = ((0, CA), (CA, WID))
ROWS = 256
ZRELS = (0, -1, 1, -2, 2, -3, 3, 4)
XRELS = (0, -1, 1, 2)


def plan():
    names = []
    for way in (1, -1):
        names += [("Bz", way, hop) for hop in (1, 2, 3, 4)]
        names += [("Ax", way, hop) for hop in (1, 2)]
        names += [("Az", way, hop, xrel) for hop in (1, 2, 3, 4) for xrel in XRELS]
        names += [("Bx", way, hop, zrel) for hop in (1, 2) for zrel in ZRELS]
    return {name: at for at, name in enumerate(names)}


NAMES = plan()
RING = {
    name: at
    for at, name in enumerate(
        [(way, hop, piece) for way in (1, -1) for hop in (1, 2, 3) for piece in (0, 1)] + [(1, 4, 0), (-1, 4, 1)]
    )
}


def remote(src, dst, send, recv, target):
    return pltpu.make_async_remote_copy(
        src_ref=src, dst_ref=dst, send_sem=send, recv_sem=recv, device_id=target, device_id_type=MESH
    )


def place():
    y = lax.axis_index("span")
    cl = lax.axis_index("clip")
    m = lax.axis_index("mp")
    return y, cl, m, cl // NZ, lax.rem(cl, NZ)


def tile_rows(r):
    return pl.ds(pl.multiple_of(r * ROWS, ROWS), ROWS)


def main_kernel(
    q_ref, k_ref, v_ref, resid_ref, w_ref, gate_ref, gain_ref, scale_ref, route_ref, len_ref, step_ref,
    out_ref, values_ref, table, most_ref,
    qkv, obuf, feats, wfull, resid, valbuf, sendbuf, ext, stage, sendx, tiles, ytiles, codes, table_s, codes_s,
    q_send, q_recv, o_send, o_recv, sib_send, sib_recv, w_send, w_recv, w_own, r_sem, v_sem,
    t_send, t_recv, t_here, y_send, y_recv, a_send, a_recv, e_send, e_recv, x_send, x_recv,
):
    y, cl, m, x, z = place()

    def clip_at(dx, dz):
        return lax.rem(x + (dx + NX), NX) * NZ + lax.rem(z + (dz + NZ), NZ)

    def first_head(yy):
        return (5 * yy + 1 - m) // 2

    def has_head(yy, i):
        return first_head(yy) + i < first_head(yy + 1)

    def cols128(at):
        return pl.ds(pl.multiple_of(at * HS, HS), HS)

    barrier = pltpu.get_barrier_semaphore()

    def greet(d, carry):
        pl.semaphore_signal(
            barrier, inc=1, device_id=(y, lax.rem(cl + d, NCLIP), m), device_id_type=MESH
        )
        return carry

    lax.fori_loop(1, NCLIP, greet, 0)
    for d in (1, 2, 3):
        pl.semaphore_signal(barrier, inc=1, device_id=(lax.rem(y + d, NY), cl, m), device_id_type=MESH)
    pl.semaphore_signal(barrier, inc=1, device_id=(y, cl, 1 - m), device_id_type=MESH)
    pl.semaphore_wait(barrier, NCLIP - 1 + 3 + 1)

    waited, sent = set(), []

    def rows_of(rel):
        return pl.ds(pl.multiple_of(clip_at(*rel) * SHARD, 16), SHARD)

    def w_start(name, rel, target, half=None, own=False):
        lo, hi = PART[name[0][0]][0 if half is None else 1 + half]
        dst = wfull.at[rows_of(rel), lo:hi]
        src = w_ref.at[:, lo:hi] if own else dst
        sent.append(hi - lo)
        remote(src, dst, w_send, w_recv.at[NAMES[name]], (y, clip_at(*target), m)).start()

    def w_wait(name, rel, half=None):
        if name in waited:
            return
        waited.add(name)
        lo, hi = PART[name[0][0]][0 if half is None else 1 + half]
        dst = wfull.at[rows_of(rel), lo:hi]
        remote(dst, dst, w_send, w_recv.at[NAMES[name]], (y, cl, m)).wait_recv()

    def half_of(way):
        return 0 if way == 1 else 1

    def bz_wait(way, hop):
        w_wait(("Bz", way, hop), (0, -way * hop), half_of(way) if hop == 4 else None)

    def ax_wait(way, hop):
        w_wait(("Ax", way, hop), (-way * hop, 0), half_of(way) if hop == 2 else None)

    def az_wait(way, hop, xrel):
        w_wait(("Az", way, hop, xrel), (xrel, -way * hop), half_of(way) if hop == 4 else None)

    def bx_wait(way, hop, zrel):
        w_wait(("Bx", way, hop, zrel), (-way * hop, zrel), half_of(way) if hop == 2 else None)

    def b_to_x(zrel, own=False):
        for way in (1, -1):
            w_start(("Bx", way, 1, zrel), (0, zrel), (way, 0), own=own)

    def a_to_z(xrel, own=False):
        for way in (1, -1):
            w_start(("Az", way, 1, xrel), (xrel, 0), (0, way), own=own)

    def bz_event(hop):
        for way in (1, -1):
            bz_wait(way, hop)
            if hop < 4:
                w_start(
                    ("Bz", way, hop + 1), (0, -way * hop), (0, way), half=half_of(way) if hop == 3 else None
                )
                b_to_x(-way * hop)
        if hop == 4:
            b_to_x(4)

    def ax_event(hop):
        for way in (1, -1):
            ax_wait(way, hop)
            if hop == 1:
                w_start(("Ax", way, 2), (-way, 0), (way, 0), half=half_of(way))
                a_to_z(-way)
        if hop == 2:
            a_to_z(2)

    def az_event(hop, xrel):
        for way in (1, -1):
            az_wait(way, hop, xrel)
            w_start(
                ("Az", way, hop + 1, xrel), (xrel, -way * hop), (0, way), half=half_of(way) if hop == 3 else None
            )

    def bx_event(zrel):
        for way in (1, -1):
            bx_wait(way, 1, zrel)
            w_start(("Bx", way, 2, zrel), (-way, zrel), (way, 0), half=half_of(way))

    def all_of(part):
        for way in (1, -1):
            if part == "A":
                for hop in (1, 2):
                    ax_wait(way, hop)
                for hop in (1, 2, 3, 4):
                    for xrel in XRELS:
                        az_wait(way, hop, xrel)
            else:
                for hop in (1, 2, 3, 4):
                    bz_wait(way, hop)
                for hop in (1, 2):
                    for zrel in ZRELS:
                        bx_wait(way, hop, zrel)

    tensors = (q_ref, k_ref, v_ref)

    def qkv_out(i, d):
        yy = lax.rem(y + d, NY)

        @pl.when(has_head(yy, i))
        def _():
            for t in range(3):
                remote(
                    tensors[t].at[:, cols128(first_head(yy) + i)],
                    qkv.at[i, y, t],
                    q_send.at[i, d],
                    q_recv.at[i, y],
                    (yy, cl, m),
                ).start()

    def qkv_here(i):
        @pl.when(has_head(y, i))
        def _():
            for t in range(3):
                pltpu.make_async_copy(
                    tensors[t].at[:, cols128(first_head(y) + i)], qkv.at[i, y, t], q_recv.at[i, y]
                ).start()

    def qkv_sent(i, d):
        yy = lax.rem(y + d, NY)

        @pl.when(has_head(yy, i))
        def _():
            remote(qkv.at[i, 0], qkv.at[i, 0], q_send.at[i, d], q_recv.at[i, 0], (yy, cl, m)).wait_send()

    def own_cols(head):
        return cols128(m * HEADS + head)

    def attend(i, c):
        @pl.when(has_head(y, i))
        def _():
            pltpu.make_async_copy(qkv.at[i, c], qkv.at[i, c], q_recv.at[i, c]).wait()

            def tile(r, carry):
                rows = tile_rows(r)
                query = qkv[i, c, 0, rows, :]
                to_two = 1.0 / (math.sqrt(HS) * math.log(2.0))
                ones = jnp.ones((TOK, HS), jnp.bfloat16)
                top = jnp.full((ROWS, 1), -jnp.inf, jnp.float32)
                acc = jnp.zeros((ROWS, 2 * HS), jnp.float32)
                for cc in range(c + 1):
                    scores = lax.dot_general(
                        query, qkv[i, cc, 1], (((1,), (1,)), ((), ())), preferred_element_type=jnp.float32
                    )
                    higher = jnp.maximum(top, jnp.max(scores, axis=1, keepdims=True))
                    prob = jnp.exp2((scores - higher) * to_two).astype(jnp.bfloat16)
                    val = jnp.concatenate([qkv[i, cc, 2], ones], axis=1)
                    acc = acc * jnp.exp2((top - higher) * to_two)
                    acc = acc + jnp.dot(prob, val, preferred_element_type=jnp.float32)
                    top = higher
                many = ROWS // BR
                done = (acc[:, :HS] / acc[:, HS:]).astype(jnp.bfloat16)
                obuf[i, c, pl.ds(r * many, many)] = done.reshape(many, BR, HS)
                return carry

            lax.fori_loop(0, TOK // ROWS, tile, 0, unroll=True)
            head = first_head(y) + i
            part = feats.at[:, :, own_cols(head)]

            @pl.when(y == c)
            def _():
                feats[:, :, own_cols(head)] = obuf[i, c]
                remote(obuf.at[i, c], part, sib_send, sib_recv, (y, cl, 1 - m)).start()

            @pl.when(y != c)
            def _():
                remote(obuf.at[i, c], part, o_send.at[i, c], o_recv.at[head], (c, cl, m)).start()

    def o_event(i):
        for d in (1, 3, 2):
            yy = lax.rem(y + d, NY)

            @pl.when(has_head(yy, i))
            def _(yy=yy):
                head = first_head(yy) + i
                part = feats.at[:, :, own_cols(head)]
                remote(part, part, o_send.at[i, 0], o_recv.at[head], (y, cl, m)).wait_recv()
                remote(part, part, sib_send, sib_recv, (y, cl, 1 - m)).start()

    def find_slots():
        shape = tiles.shape[1:]
        row_at = lax.broadcasted_iota(jnp.int32, shape, 0)
        group = lax.broadcasted_iota(jnp.int32, shape, 1)
        first = jnp.full(shape, NB, jnp.int32)
        second = jnp.full(shape, NB, jnp.int32)
        for b in range(NB):
            here = group == route_ref[b]
            second = jnp.where(here & (first < NB) & (second == NB), b, second)
            first = jnp.where(here & (first == NB), b, first)
        have = jnp.where(second < NB, 1, 0)
        upto = have
        for shift in (1, 2, 4, 8, 16):
            upto = upto + jnp.where(group >= shift, pltpu.roll(upto, shift, 1), 0)
        before = upto - have
        total = jnp.sum(have, axis=1, keepdims=True)
        code = jnp.where((have == 1) & (before < CAP), before, CAP)
        extra = jnp.zeros(shape, jnp.int32)
        for e in range(CAP):
            at = jnp.sum(jnp.where((have == 1) & (before == e), second, 0), axis=1, keepdims=True)
            extra = jnp.where(group == e, at, extra)
        table[...] = jnp.where(row_at == 0, first, jnp.where(row_at == 1, second, extra))
        tiles[cl] = jnp.where(row_at == 0, code, total)

        def tell(d, carry):
            g = lax.rem(cl + d, NCLIP)
            remote(tiles.at[cl], tiles.at[cl], t_send, t_recv, (y, g, m)).start()
            return carry

        lax.fori_loop(1, NCLIP, tell, 0)
        table_copy.start()

    def share_most():
        others = tiles.at[0 : NCLIP - 1]
        remote(others, others, t_send, t_recv, (y, cl, m)).wait_recv()
        codes[...] = tiles[:, 0, :]
        codes_copy.start()
        ytiles[y] = jnp.max(tiles[:, 1:2, :], axis=0) + jnp.zeros((8, 128), jnp.int32)
        for d in (1, 2, 3):
            remote(ytiles.at[y], ytiles.at[y], y_send.at[d], y_recv.at[y], (lax.rem(y + d, NY), cl, m)).start()

    def know_most():
        for d in (1, 2, 3):
            yy = lax.rem(y + d, NY)
            remote(ytiles.at[yy], ytiles.at[yy], y_send.at[d], y_recv.at[yy], (y, cl, m)).wait_recv()
        most_ref[0, 0] = jnp.max(ytiles[...])

    table_copy = pltpu.make_async_copy(table, table_s, t_here.at[0])
    codes_copy = pltpu.make_async_copy(codes, codes_s, t_here.at[1])

    w_start(("Bz", 1, 1), (0, 0), (0, 1), own=True)
    w_start(("Bz", -1, 1), (0, 0), (0, -1), own=True)
    for way in (1, -1):
        w_start(("Ax", way, 1), (0, 0), (way, 0), own=True)
    b_to_x(0, own=True)
    for i in range(MAXH):
        for d in (1, 3, 2):
            qkv_out(i, d)
        qkv_here(i)
        if i == 0:
            a_to_z(0, own=True)
    w_copy = pltpu.make_async_copy(w_ref, wfull.at[rows_of((0, 0)), :], w_own)
    w_copy.start()
    resid_copy = pltpu.make_async_copy(resid_ref, resid, r_sem)
    resid_copy.start()
    valbuf[NB] = jnp.zeros((BR, WID), jnp.bfloat16)
    stage[CAP] = jnp.zeros((BR, WID), jnp.bfloat16)

    events = [(1.0, find_slots), (24.0, share_most), (32.0, know_most)]
    for hop, at in ((1, 5.5), (2, 11.0), (3, 16.5), (4, 20.0)):
        events.append((at, functools.partial(bz_event, hop)))
    for hop, at in ((1, 4.0), (2, 7.0)):
        events.append((at, functools.partial(ax_event, hop)))
    for hop in (1, 2, 3):
        for n, xrel in enumerate(XRELS):
            events.append((17.0 + 13.0 * (hop - 1) + 3.3 * n, functools.partial(az_event, hop, xrel)))
    for n, zrel in enumerate(ZRELS):
        events.append((7.6 * (n + 1), functools.partial(bx_event, zrel)))
    for i, at, back in ((0, 17.0, 27.0), (1, 35.0, 45.0), (2, 50.0, 61.0)):
        for c in range(NY):
            events.append((at + 0.7 * c, functools.partial(attend, i, c)))
        events.append((back, functools.partial(o_event, i)))
    events.sort(key=lambda item: item[0])
    late = [act for at, act in events if at > 61.0]
    for at, act in events:
        if at <= 61.0:
            act()

    half_feats = feats.at[:, :, pl.ds(pl.multiple_of((1 - m) * HALF, HS), HALF)]
    remote(half_feats, half_feats, sib_send, sib_recv, (y, cl, 1 - m)).wait_recv()
    w_copy.wait()
    resid_copy.wait()
    table_copy.wait()
    codes_copy.wait()

    step, factor = step_and_factor(step_ref, len_ref, scale_ref, cl, y)

    def project(n):
        lo, hi, part = CHUNKS[n]
        all_of(part)
        many = ROWS // BR

        def tile(r, carry):
            blocks = pl.ds(r * many, many)
            feat = feats[blocks].reshape(ROWS, INNER)
            proj = jnp.dot(feat, wfull[:, lo:hi], preferred_element_type=jnp.float32)
            gate = gate_ref[pl.ds(step, 1), lo:hi]
            left = resid[blocks, :, lo:hi].reshape(ROWS, hi - lo).astype(jnp.float32)
            row = (left + gate * proj).astype(jnp.bfloat16)
            value = (row.astype(jnp.float32) * factor * gain_ref[lo:hi].reshape(1, hi - lo)).astype(jnp.bfloat16)
            valbuf[blocks, :, lo:hi] = value.reshape(many, BR, hi - lo)
            return carry

        lax.fori_loop(0, TOK // ROWS, tile, 0)

    def firsts(n):
        lo, hi, part = CHUNKS[n]

        def send(d, carry):
            g = lax.rem(cl + d, NCLIP)
            sendbuf[g, :, lo:hi] = valbuf[table_s[0, g], :, lo:hi]
            remote(
                sendbuf.at[g, :, lo:hi], out_ref.at[cl, 0, :, lo:hi], a_send.at[n], a_recv.at[n], (y, g, m)
            ).start()
            return carry

        lax.fori_loop(1, NCLIP, send, 0)
        sendbuf[cl, :, lo:hi] = valbuf[table_s[0, cl], :, lo:hi]
        pltpu.make_async_copy(sendbuf.at[cl, :, lo:hi], out_ref.at[cl, 0, :, lo:hi], a_recv.at[n]).start()

    def z_at(dz):
        return lax.rem(z + (dz + NZ), NZ)

    def ring_start(way, hop, piece):
        lo, hi = PIECES[piece]
        part = ext.at[z_at(-way * (hop - 1)), :, :, lo:hi]
        remote(part, part, e_send, e_recv.at[RING[way, hop, piece]], (y, clip_at(0, way), m)).start()

    def ring_wait(way, hop, piece):
        lo, hi = PIECES[piece]
        part = ext.at[z_at(-way * hop), :, :, lo:hi]
        remote(part, part, e_send, e_recv.at[RING[way, hop, piece]], (y, cl, m)).wait_recv()

    def seconds(piece):
        lo, hi = PIECES[piece]
        for e in range(CAP):
            ext[z, e, :, lo:hi] = valbuf[table_s[2, e], :, lo:hi]
        for way in (1, -1):
            ring_start(way, 1, piece)

    def ring_event(hop, piece):
        for way in (1, -1):
            if (way, hop, piece) in RING:
                ring_wait(way, hop, piece)
                if (way, hop + 1, piece) in RING:
                    ring_start(way, hop + 1, piece)

    def to_x(zrel):
        zs = z_at(zrel)
        source = x * NZ + zs
        stage[0:CAP] = ext[zs]
        for d in (1, 3, 2, 0):
            xx = lax.rem(x + d, NX)
            g = xx * NZ + z
            sendx[xx, zs] = stage[codes_s[source, g]]
            if d:
                remote(sendx.at[xx, zs], out_ref.at[source, 1], x_send, x_recv, (y, g, m)).start()
            else:
                pltpu.make_async_copy(sendx.at[xx, zs], out_ref.at[source, 1], x_recv).start()

    def next_late(many):
        for _ in range(many):
            if late:
                late.pop(0)()

    project(0)
    firsts(0)
    next_late(1)
    project(1)
    seconds(0)
    firsts(1)
    next_late(len(late))
    project(2)
    project(3)
    project(4)
    seconds(1)
    values_copy = pltpu.make_async_copy(valbuf.at[0:NB], values_ref, v_sem)
    values_copy.start()
    to_x(0)
    ring_event(1, 0)
    firsts(2)
    ring_event(1, 1)
    to_x(1)
    to_x(-1)
    ring_event(2, 0)
    firsts(3)
    ring_event(2, 1)
    to_x(2)
    to_x(-2)
    ring_event(3, 0)
    firsts(4)
    ring_event(3, 1)
    to_x(3)
    to_x(-3)
    ring_event(4, 0)
    ring_event(4, 1)
    to_x(4)

    assert len(waited) == len(NAMES) and sum(sent) == (NCLIP - 1) * WID and not late
    for n, (lo, hi, part) in enumerate(CHUNKS):
        most = sendbuf.at[0 : NCLIP - 1, :, lo:hi]
        remote(most, most, a_send.at[n], a_recv.at[n], (y, cl, m)).wait_send()
        whole = out_ref.at[:, 0, :, lo:hi]
        pltpu.make_async_copy(whole, whole, a_recv.at[n]).wait()
    most = ext.at[0 : NZ - 1]
    remote(most, most, e_send, e_recv.at[0], (y, cl, m)).wait_send()
    most = sendx.at[0 : NX - 1]
    remote(most, most, x_send, x_recv, (y, cl, m)).wait_send()
    whole = out_ref.at[:, 1]
    pltpu.make_async_copy(whole, whole, x_recv).wait()
    values_copy.wait()
    remote(half_feats, half_feats, sib_send, sib_recv, (y, cl, 1 - m)).wait_send()
    most = wfull.at[0 : (NCLIP - 1) * SHARD, :]
    remote(most, most, w_send, w_recv.at[0], (y, cl, m)).wait_send()
    others = tiles.at[0 : NCLIP - 1]
    remote(others, others, t_send, t_recv, (y, cl, m)).wait_send()
    for d in (1, 2, 3):
        remote(ytiles.at[0], ytiles.at[0], y_send.at[d], y_recv.at[0], (y, cl, m)).wait_send()
    for i in range(MAXH):
        for d in (1, 2, 3):
            qkv_sent(i, d)
        for c in range(NY):

            @pl.when(has_head(y, i) & (y != c))
            def _(i=i, c=c):
                remote(obuf.at[i, c], obuf.at[i, c], o_send.at[i, c], o_recv.at[0], (y, cl, m)).wait_send()


def step_and_factor(step_ref, len_ref, scale_ref, cl, y):
    step = step_ref[y, cl]
    live = jnp.where(y < len_ref[cl], 1.0, 0.0).astype(jnp.float32)
    return step, scale_ref[step] * live


def second_kernel(values_ref, table, out_ref, valbuf, sendbuf, v_sem, a_send, a_recv):
    y, cl, m, x, z = place()
    barrier = pltpu.get_barrier_semaphore()

    def greet(d, carry):
        pl.semaphore_signal(
            barrier, inc=1, device_id=(y, lax.rem(cl + d, NCLIP), m), device_id_type=MESH
        )
        return carry

    lax.fori_loop(1, NCLIP, greet, 0)
    load = pltpu.make_async_copy(values_ref, valbuf.at[0:NB], v_sem)
    load.start()
    load.wait()
    valbuf[NB] = jnp.zeros((BR, WID), jnp.bfloat16)
    pl.semaphore_wait(barrier, NCLIP - 1)

    def send(d, carry):
        g = lax.rem(cl + d, NCLIP)
        sendbuf[g] = valbuf[table[1, g]]
        remote(sendbuf.at[g], out_ref.at[cl], a_send, a_recv, (y, g, m)).start()
        return carry

    lax.fori_loop(1, NCLIP, send, 0)
    sendbuf[cl] = valbuf[table[1, cl]]
    pltpu.make_async_copy(sendbuf.at[cl], out_ref.at[cl], a_recv).start()
    most = sendbuf.at[0 : NCLIP - 1]
    remote(most, most, a_send, a_recv, (y, cl, m)).wait_send()
    pltpu.make_async_copy(out_ref, out_ref, a_recv).wait()


def shards(queries, keys, values, resid, out_weight, gate_table, step_scale, gain, route, clip_len, tstep):
    any_place = pl.BlockSpec(memory_space=pl.ANY)
    hbm = pl.BlockSpec(memory_space=pltpu.HBM)
    vmem = pl.BlockSpec(memory_space=pltpu.VMEM)
    smem = pl.BlockSpec(memory_space=pltpu.SMEM)
    dma = pltpu.SemaphoreType.DMA
    bf16, i32 = jnp.bfloat16, jnp.int32
    shape = jax.ShapeDtypeStruct
    scored, rows, table, most = pl.pallas_call(
        main_kernel,
        out_shape=(
            shape((NCLIP, 2, BR, WID), bf16),
            shape((NB, BR, WID), bf16),
            shape((8, 128), i32),
            shape((1, 1), i32),
        ),
        in_specs=[hbm] * 5 + [vmem] * 2 + [smem] * 4,
        out_specs=(any_place, hbm, vmem, smem),
        scratch_shapes=[
            pltpu.VMEM((MAXH, NY, 3, TOK, HS), bf16),
            pltpu.VMEM((MAXH, NY, NB, BR, HS), bf16),
            pltpu.VMEM((NB, BR, INNER), bf16),
            pltpu.VMEM((INNER, WID), bf16),
            pltpu.VMEM((NB, BR, WID), bf16),
            pltpu.VMEM((NB + 1, BR, WID), bf16),
            pltpu.VMEM((NCLIP, BR, WID), bf16),
            pltpu.VMEM((NZ, CAP, BR, WID), bf16),
            pltpu.VMEM((CAP + 1, BR, WID), bf16),
            pltpu.VMEM((NX, NZ, BR, WID), bf16),
            pltpu.VMEM((NCLIP, 8, 128), i32),
            pltpu.VMEM((NY, 8, 128), i32),
            pltpu.VMEM((NCLIP, 128), i32),
            pltpu.SMEM((8, 128), i32),
            pltpu.SMEM((NCLIP, 128), i32),
            dma((MAXH, NY)),
            dma((MAXH, NY)),
            dma((MAXH, NY)),
            dma((HEADS,)),
            dma,
            dma,
            dma,
            dma((len(NAMES),)),
            dma,
            dma,
            dma,
            dma,
            dma,
            dma((2,)),
            dma((NY,)),
            dma((NY,)),
            dma((len(CHUNKS),)),
            dma((len(CHUNKS),)),
            dma,
            dma((len(RING),)),
            dma,
            dma,
        ],
        compiler_params=pltpu.CompilerParams(
            collective_id=0, has_side_effects=True, vmem_limit_bytes=58 * 1024 * 1024
        ),
        cost_estimate=pl.CostEstimate(flops=11_000_000_000, bytes_accessed=40_000_000, transcendentals=8_000_000),
    )(
        queries[0, 0],
        keys[0, 0],
        values[0, 0],
        resid[0, 0].reshape(NB, BR, WID),
        out_weight,
        gate_table,
        gain,
        step_scale,
        route[0, 0, :, 0],
        clip_len,
        tstep.T,
    )

    def direct(scored, rows, table):
        second = pl.pallas_call(
            second_kernel,
            out_shape=shape((NCLIP, BR, WID), bf16),
            in_specs=[hbm, smem],
            out_specs=hbm,
            scratch_shapes=[
                pltpu.VMEM((NB + 1, BR, WID), bf16),
                pltpu.VMEM((NCLIP, BR, WID), bf16),
                dma,
                dma,
                dma,
            ],
            compiler_params=pltpu.CompilerParams(
                collective_id=1, has_side_effects=True, vmem_limit_bytes=16 * 1024 * 1024
            ),
        )(rows, table)
        return jnp.concatenate([scored[:, :1], second[:, None]], axis=1)

    scored = lax.cond(most[0, 0] <= CAP, lambda scored, rows, table: scored, direct, scored, rows, table)
    return scored[None, None]


def solution(mesh):
    placed = (
        P("clip", "span", None, "mp"),
        P("clip", "span", None, "mp"),
        P("clip", "span", None, "mp"),
        P("clip", "span", None, "mp"),
        P("clip", "mp"),
        P(None, "mp"),
        P(),
        P("mp"),
        P("clip", "span", None, None),
        P(),
        P(),
    )
    return jax.shard_map(
        shards,
        mesh=mesh,
        in_specs=placed,
        out_specs=P("span", "clip", None, None, None, "mp"),
        check_vma=False,
    )
```
